512 devices in a mesh: seq: 64 (over y, z), slide: 8 (over x, core).
Axes of the slice: x: 4, y: 4, z: 16, core: 2. Of those that a mesh axis runs over, the one named last changes fastest.
Arguments:
- queries: bfloat16 [8, 16384, 1024], P('slide', 'seq'), may hold values from -8 to 8
- key_rows: bfloat16 [8, 16384, 1024], P('slide', 'seq'), may hold values from -8 to 8
- values: bfloat16 [8, 16384, 1024], P('slide', 'seq'), may hold values from -8 to 8
- tissue: int32 [8, 128], P('slide', 'seq'), may hold values 0 or 1
- routes: int32 [8, 1024, 4], P('slide', 'seq'), may hold values from 0 to 63, all different within a row; in each aligned block of 16 rows (0 to 15, 16 to 31, ..., all dimensions but the last counted through in order) at most 2 rows name the same one
Outputs:
- attended: bfloat16 [8, 16384, 1024], P('slide', 'seq')
The draws below stay inside these ranges and needn't reach their ends.
Inputs may be any that keep to these rules, and one draw needn't show every extreme that they name: `routes`: row t*8 + g belongs to query tile t and pair g; each row names 4 different key blocks; among the rows of one key block (16 rows) no block is named more than 2 times, and some block is named exactly 2 times.
All inputs are finite; a program needn't handle non-finite values. No bound on the sum of `tissue` on one device may be relied on, other than what follows from the above.
Results may differ from the reference program's by a relative error of at most 0.0058.
Values may be sent and summed in bfloat16 or wider, within the bound.
A program may use at most 64 MiB of HBM per device.

```python
import math
import jax
import jax.numpy as jnp
import numpy as np
from jax import lax

D = 1024
E = 64
TILE = 128
SPAN = 4
TOK_DEV = 256
HP = 8
TILES_DEV = 2
UNITS_DEV = 16
CAP = 2
TOKENS = 16384
TILES = 128
SLIDES = 8
N_SEQ = 64


def draw_queries(key, part):
    key = jax.random.fold_in(key, 3)
    drawn = 2.0 * jnp.clip(jax.random.normal(key, (SLIDES, TOKENS, D), jnp.float32), -4.0, 4.0)
    return drawn.astype(jnp.bfloat16)


def draw_key_rows(key, part):
    key = jax.random.fold_in(key, 5)
    drawn = jnp.clip(jax.random.normal(key, (SLIDES, TOKENS, D), jnp.float32), -6.0, 6.0)
    return drawn.astype(jnp.bfloat16)


def with_ends(values, stream_key, low, largest):
    longest = values.shape.index(max(values.shape))
    spots = []
    for shift in (0, 1):
        where = [jax.random.randint(jax.random.fold_in(stream_key, axis), (), 0, length) for axis, length in enumerate(values.shape)]
        where[longest] = (where[longest] + shift) % values.shape[longest]
        spots.append(tuple(where))
    return values.at[spots[0]].set(low).at[spots[1]].set(largest)


def steps_of(own_key, shape, cuts, least, largest):
    def one(dim, blocks):
        draws = jax.random.uniform(jax.random.fold_in(jax.random.fold_in(own_key, 6), dim), (blocks,), jnp.float32, least / len(cuts), largest / len(cuts))
        return jnp.repeat(jnp.exp(draws), shape[dim] // blocks).reshape((-1,) + (1,) * (len(shape) - dim - 1))

    factor_of = one(*cuts[0])
    for cut in cuts[1:]:
        factor_of = factor_of * one(*cut)
    return factor_of


def assign_block(stream_key, own, number, rows, count, top, reach, lean):
    order = jax.random.permutation(stream_key, count)
    heavy_load, common = shares(count, rows * top, reach, lean, True), shares(count, rows * top, reach, lean, False)
    places = jnp.arange(count)

    def named(lengths, rotation):
        used = int((lengths > 0).sum())
        fixed = max(1, used // 4)
        shifted = fixed + (places - fixed + rotation * (used - fixed)) % max(1, count - fixed)
        return jnp.zeros((count,), jnp.int32).at[order[jnp.where(places < fixed, places, shifted)]].set(jnp.asarray(lengths, jnp.int32))

    lengths = jnp.where(number % 4 == 0, named(heavy_load, number // 4), named(common, number - number // 4 - 1))
    mixed = jax.random.permutation(jax.random.fold_in(own, 3), count)
    source_of, taker = mixed[0:count // 2 * 2:2], mixed[1:count // 2 * 2:2]
    room = jnp.minimum(lengths[source_of] - 1, reach - lengths[taker]) // 2
    room = jnp.where((source_of == order[0]) | (taker == order[0]) | (lengths[taker] == 0), 0, jnp.maximum(room, 0))
    shifted = jax.random.randint(jax.random.fold_in(own, 4), (count // 2,), 0, 1 << 20) % (room + 1)
    lengths = lengths.at[source_of].add(-shifted).at[taker].add(shifted)
    members = jnp.searchsorted(jnp.cumsum(lengths), jnp.arange(rows * top), side="right").astype(jnp.int32)
    listing = members.reshape(top, rows).T
    listing = listing[jax.random.permutation(jax.random.fold_in(own, 1), rows)]
    rotation = jax.random.randint(jax.random.fold_in(own, 2), (rows, 1), 0, top)
    return jnp.take_along_axis(listing, (jnp.arange(top)[None, :] + rotation) % top, axis=1)


def shares(number_of, total, reach, skew, full):
    loads = [(1 << 20) // math.isqrt(rank ** skew) + 1 for rank in range(1, number_of + 1)]
    largest = reach if full else min(reach, max(-(-total // number_of), total * loads[0] // sum(loads)))
    least = 1 if total - largest >= number_of - 1 else 0
    given, surplus = [largest] + [least] * (number_of - 1), total - largest - least * (number_of - 1)
    while surplus > 0:
        movable = [i for i in range(1, number_of) if given[i] < largest] or [i for i in range(1, number_of) if given[i] < reach]
        pool, budget = sum([loads[i] for i in movable]), surplus
        for i in movable:
            extra = min(reach - given[i], max(1, budget * loads[i] // pool), surplus)
            given[i] = given[i] + extra
            surplus = surplus - extra
    return np.array(given)


def noise(rng, dims, width, bound, cuts=(), kind=jnp.bfloat16):
    loudness = steps_of(rng, dims, cuts, -0.22, 0.18) if cuts else 1.0
    array = jax.random.normal(rng, dims, jnp.float32) * width * loudness
    return jnp.minimum(jnp.maximum(array, -bound), bound).astype(kind)


def setup_inputs(seed: int = 0) -> dict:
    key_of = jax.random.split(jax.random.key(seed), 6)
    queries = draw_queries(jax.random.fold_in(key_of[5], 71), 0)
    key_rows = draw_key_rows(jax.random.fold_in(key_of[5], 71), 0)
    values = noise(key_of[2], (SLIDES, TOKENS, D), 2.0, 8.0, ((0, 8), (1, 64)))
    tissue = with_ends((jax.random.randint(key_of[3], (SLIDES, TILES), 0, 4) < 3).astype(jnp.int32), jax.random.fold_in(key_of[3], 1), 0, 1)
    routes_keys = jax.random.split(jax.random.fold_in(key_of[4], 1), SLIDES * (TILES * HP) // UNITS_DEV)
    routes_turns = jax.random.permutation(jax.random.fold_in(key_of[4], 3), SLIDES * (TILES * HP) // UNITS_DEV)
    routes = jax.vmap(lambda own, number: assign_block(jax.random.fold_in(key_of[4], 2), own, number, UNITS_DEV, N_SEQ, SPAN, CAP, 2))(routes_keys, routes_turns).reshape((SLIDES, TILES * HP, SPAN))
    return {"queries": queries, "key_rows": key_rows, "values": values, "tissue": tissue, "routes": routes}


big_negative = -1.0e30


def rounded(values):
    return lax.optimization_barrier(values.astype(jnp.bfloat16)).astype(jnp.float32)


def reference(queries, key_rows, values, tissue, routes):
    score_scale = E ** -0.5

    def one_slide(slide_parts):
        slide_q, slide_k, slide_v, slide_tissue, slide_routes = slide_parts
        q_units = slide_q.reshape(TILES, TILE, HP, 2, E)
        k_units = slide_k.reshape(TILES, TILE, HP, 2, E)
        v_units = slide_v.reshape(TILES, TILE, HP, 2, E)
        k_blocks = slide_k.reshape(N_SEQ, TOK_DEV, HP, 2, E).transpose(2, 0, 1, 3, 4)
        v_blocks = slide_v.reshape(N_SEQ, TOK_DEV, HP, 2, E).transpose(2, 0, 1, 3, 4)
        key_offsets = jnp.arange(TOK_DEV, dtype=jnp.int32) // TILE
        pair_index = jnp.arange(HP, dtype=jnp.int32)

        def one_tile(tile_index):
            query_tile = q_units[tile_index].astype(jnp.float32)
            own_keys = k_units[tile_index].astype(jnp.float32)
            own_values = v_units[tile_index].astype(jnp.float32)
            own_scores = jnp.einsum("qghe,kghe->ghqk", query_tile, own_keys) * score_scale
            own_shift = jnp.max(own_scores, axis=-1)
            own_probs = jnp.exp(own_scores - own_shift[..., None])
            own_total = jnp.sum(own_probs, axis=-1)
            own_partial = jnp.einsum("ghqk,kghe->ghqe", rounded(own_probs), own_values)
            listed = lax.dynamic_slice_in_dim(slide_routes, tile_index * HP, HP, 0)
            chosen_keys = k_blocks[pair_index[:, None], listed].astype(jnp.float32)
            chosen_values = v_blocks[pair_index[:, None], listed].astype(jnp.float32)
            key_tiles = listed[:, :, None] * TILES_DEV + key_offsets[None, None, :]
            usable = (slide_tissue[key_tiles] == 1) & (key_tiles != tile_index)
            key_mask = usable[:, :, None, None, :]
            scores = jnp.einsum("qghe,gjkhe->gjhqk", query_tile, chosen_keys) * score_scale
            scores = jnp.where(key_mask, scores, big_negative)
            shift_max = rounded(jnp.max(scores, axis=-1))
            weights = jnp.where(key_mask, jnp.exp(scores - shift_max[..., None]), jnp.float32(0.0))
            total_sum = rounded(jnp.sum(weights, axis=-1))
            partial_value = rounded(jnp.einsum("gjhqk,gjkhe->gjhqe", rounded(weights), chosen_values))
            highest = jnp.maximum(own_shift, jnp.max(shift_max, axis=1))
            own_weight = jnp.exp(own_shift - highest)
            listed_weight = jnp.exp(shift_max - highest[:, None])
            numerator = own_weight[..., None] * own_partial + jnp.sum(listed_weight[..., None] * partial_value, axis=1)
            denominator = own_weight * own_total + jnp.sum(listed_weight * total_sum, axis=1)
            result = numerator / denominator[..., None]
            return result.transpose(2, 0, 1, 3).reshape(TILE, HP * 2 * E).astype(jnp.bfloat16)

        tiles_out = lax.map(one_tile, jnp.arange(TILES, dtype=jnp.int32))
        return tiles_out.reshape(TOKENS, HP * 2 * E)

    return lax.map(one_slide, (queries, key_rows, values, tissue, routes))
```

```python
import jax
import jax.numpy as jnp
from jax import lax
from jax.experimental import pallas as pl
from jax.experimental.pallas import tpu as pltpu
from jax.sharding import PartitionSpec as P

NY = 4
NZ = 16
TILE = 128
HP = 8
PAIR = 128
HALF = NZ // 2
WINDOW = HP // 2
UNITS = 16
SPAN = 4
ROWS = 144

big_negative = -1e30
MESH = pl.DeviceIdType.MESH


def halves(unit):
    mid = PAIR // 2
    zero = jnp.zeros((mid, TILE), unit.dtype)
    upper = jnp.concatenate([unit[:mid], zero], axis=1)
    return jnp.concatenate([upper, jnp.concatenate([zero, unit[mid:]], axis=1)], axis=0)


def fold(both):
    mid = PAIR // 2
    return jnp.concatenate([both[:mid, :TILE], both[mid:, TILE:]], axis=0)


def by_head(pair_row):
    return pair_row[:, :TILE], pair_row[:, TILE:]


def kernel(
    tissue_hbm, routes_hbm, q_hbm, k_hbm, v_hbm, out,
    tissue, routes, q_rows, k_rows, v_rows, kv, tis, work_o, work_r, work_l, qs, tab, tabv, tabs, tabo, places,
    ret_out, ret_in, own_acc, own_stat,
    rs, rr, ls, lr, trs, trr, tls, tlr, q_send, q_recv, t_send, t_recv, ret_s, ret_r, loc,
):
    me = lax.axis_index("seq")
    y, z = me // NZ, me % NZ

    loads = [
        pltpu.make_async_copy(k_hbm.at[0], k_rows, loc.at[0]),
        pltpu.make_async_copy(v_hbm.at[0], v_rows, loc.at[1]),
        pltpu.make_async_copy(q_hbm.at[0], q_rows, loc.at[2]),
        pltpu.make_async_copy(routes_hbm.at[0], routes, loc.at[5]),
        pltpu.make_async_copy(tissue_hbm, tissue, loc.at[6]),
    ]
    for load in loads:
        load.start()

    def at(row, column):
        return {"seq": row % NY * NZ + column % NZ}

    right, left = at(y, z + 1), at(y, z + NZ - 1)

    def peer(dy):
        return at(y + dy, z)

    def remote(src, dst, send, recv, device):
        return pltpu.make_async_remote_copy(
            src_ref=src, dst_ref=dst, send_sem=send, recv_sem=recv,
            device_id=device, device_id_type=MESH,
        )

    barrier = pltpu.get_barrier_semaphore()
    for device in [right, left] + [peer(dy) for dy in range(1, NY)]:
        pl.semaphore_signal(barrier, inc=1, device_id=device, device_id_type=MESH)

    def chunk_right(s, c):
        return remote(kv.at[s - 1, c], kv.at[s, c], rs.at[s, c], rr.at[s, c], right)

    def chunk_left(s, c):
        pair = (c + WINDOW) % HP
        return remote(
            kv.at[(NZ + 1 - s) % NZ, pair], kv.at[NZ - s, pair], ls.at[s, c], lr.at[s, c], left
        )

    def tis_right(s):
        return remote(tis.at[s - 1], tis.at[s], trs.at[s], trr.at[s], right)

    def tis_left(s):
        return remote(tis.at[(NZ + 1 - s) % NZ], tis.at[NZ - s], tls.at[s], tlr.at[s], left)

    def tab_copy(dy):
        back = (NY - dy) % NY
        return remote(tab.at[dy], tabv.at[back], t_send.at[dy], t_recv.at[back], peer(dy))

    half = UNITS // 2

    def q_up(part):
        units = pl.ds(part * half, half)
        return remote(qs.at[0, units], qs.at[NY - 1, units], q_send.at[0, part], q_recv.at[0, part], peer(1))

    def q_down(part):
        units = pl.ds(part * half, half)
        return remote(qs.at[0, units], qs.at[1, units], q_send.at[1, part], q_recv.at[1, part], peer(NY - 1))

    def q_on_up():
        units = pl.ds(0, half)
        return remote(qs.at[NY - 1, units], qs.at[2, units], q_send.at[2, 0], q_recv.at[2, 0], peer(1))

    def q_on_down():
        units = pl.ds(half, half)
        return remote(qs.at[1, units], qs.at[2, units], q_send.at[2, 1], q_recv.at[2, 1], peer(NY - 1))

    def lay_pair(g):
        columns = slice(g * PAIR, (g + 1) * PAIR)
        for t in range(2):
            tokens = slice(t * TILE, (t + 1) * TILE)
            kv[0, g, t] = k_rows[tokens, columns]
            kv[0, g, 2 + t] = v_rows[tokens, columns].T

    loads[0].wait()
    loads[1].wait()
    for c in range(WINDOW):
        lay_pair(c)
        lay_pair(c + WINDOW)
        if c == 0:
            pl.semaphore_wait(barrier, 2 + NY - 1)
        chunk_right(1, c).start()
        chunk_left(1, c).start()

    for load in loads[3:]:
        load.wait()
    for t in range(2):
        tis[0, t] = jnp.full((8, 128), (tissue[0, t] == 1).astype(jnp.int32), jnp.int32)
    tis_right(1).start()
    tis_left(1).start()

    lane = lax.broadcasted_iota(jnp.int32, (8, 128), 1)
    row = lax.broadcasted_iota(jnp.int32, (8, 128), 0)
    block = (y + row) % NY * NZ + (z + NZ - (lane // 2) % NZ) % NZ
    first = jnp.full((8, 128), UNITS - 1, jnp.int32)
    last = jnp.zeros((8, 128), jnp.int32)
    for u in range(UNITS):
        named = block == routes[0, u]
        for j in range(1, SPAN):
            named = named | (block == routes[j, u])
        first = jnp.where(named, jnp.minimum(first, u), first)
        last = jnp.where(named, u, last)
    table = jnp.where(lane % 2 == 0, first, last)
    for dy in range(NY):
        tab[dy] = jnp.broadcast_to(table[dy : dy + 1], (8, 128))
    for dy in range(1, NY):
        tab_copy(dy).start()

    scale = jnp.bfloat16((PAIR // 2) ** -0.5)
    loads[2].wait()

    def lay_queries(part):
        for i in range(half):
            u = part * half + i
            tile, g = u // HP, u % HP
            qs[0, u] = (q_rows[tile * TILE : (tile + 1) * TILE, g * PAIR : (g + 1) * PAIR] * scale).T

    lay_queries(0)
    q_up(0).start()
    lay_queries(1)
    q_down(1).start()
    q_up(1).start()
    q_down(0).start()

    def own_units(low, count):
        numbers = [low + i for i in range(count)]

        def scores_of(u):
            return jnp.dot(
                kv[0, u % HP, u // HP], halves(qs[0, u]), preferred_element_type=jnp.float32
            )

        scores = scores_of(numbers[0])
        done = []
        for i, u in enumerate(numbers):
            later = scores_of(numbers[i + 1]) if i + 1 < count else None
            shift = jnp.max(scores, axis=0, keepdims=True)
            probs = jnp.exp(scores - shift)
            total = jnp.sum(probs, axis=0, keepdims=True)
            both = jnp.dot(
                kv[0, u % HP, 2 + u // HP], probs.astype(jnp.bfloat16), preferred_element_type=jnp.float32
            )
            done.append((u, fold(both), by_head(shift) + by_head(total)))
            scores = later
        for u, folded, four in done:
            own_acc[u] = folded
            own_stat[u] = jnp.concatenate(four + four, axis=0)

    def slots(jobs):
        def scores_of(job):
            work, d, dy, c = job
            u = tabs[dy, 0, d * 2 + c]
            g = u & (HP - 1)
            unit = halves(qs[dy, u])
            keep = []
            for t in range(2):
                row = tis[d, t, 0:1, :]
                if work is work_o:
                    row = row * (1 - ((dy == 0) & ((u >> 3) == t)).astype(jnp.int32))
                keep.append(jnp.concatenate([row, row], axis=1) != 0)
            value = jnp.concatenate([work[g, 2], work[g, 3]], axis=1)
            keys = jnp.concatenate([work[g, 0], work[g, 1]], axis=0)
            both = jnp.dot(keys, unit, preferred_element_type=jnp.float32)
            return [both[:TILE], both[TILE:]], keep, value

        ready = scores_of(jobs[0])
        done = []
        for i, job in enumerate(jobs):
            later = scores_of(jobs[i + 1]) if i + 1 < len(jobs) else None
            scores, keep, value = ready
            peaks = [
                jnp.where(keep[t], jnp.max(scores[t], axis=0, keepdims=True), big_negative)
                for t in range(2)
            ]
            shift = jnp.maximum(peaks[0], peaks[1]).astype(jnp.bfloat16).astype(jnp.float32)
            weights = [
                jnp.exp(scores[t] - jnp.where(keep[t], shift, -big_negative)) for t in range(2)
            ]
            total = jnp.sum(weights[0], axis=0, keepdims=True) + jnp.sum(weights[1], axis=0, keepdims=True)
            both = jnp.dot(
                value,
                jnp.concatenate([w.astype(jnp.bfloat16) for w in weights], axis=0),
                preferred_element_type=jnp.float32,
            )
            four = by_head(shift) + by_head(total)
            done.append((job, fold(both), jnp.concatenate(four * 4, axis=0)))
            ready = later
        for (work, d, dy, c), folded, stat in done:
            ret_out[dy, d, c, 0:PAIR, :] = folded.astype(jnp.bfloat16)
            ret_out[dy, d, c, PAIR:ROWS, :] = stat.astype(jnp.bfloat16)

    def ret_copy(dy, d):
        back = (NY - dy) % NY
        return remote(
            ret_out.at[dy, d], ret_in.at[back * NZ + d], ret_s.at[dy, d], ret_r.at[back, d], peer(dy)
        )

    def ret_local(d):
        return pltpu.make_async_copy(ret_out.at[0, d], ret_in.at[d], ret_r.at[0, d])

    def give_back(dy, d):
        @pl.when(dy == 0)
        def _():
            ret_local(d).start()

        @pl.when(dy > 0)
        def _():
            ret_copy(dy, d).start()

    def ret_wait(d):
        ret_local(d).wait()
        for dy in range(1, NY):
            ret_copy(dy, d).wait_send()
            ret_copy(dy, d).wait_recv()

    def fill(work, d):
        for g in range(HP):
            work[g] = kv[d, g]

    def relay(s, c):
        later, chunk = s + (c + WINDOW) // HP, (c + WINDOW) % HP
        chunk_right(s, c).wait_send()
        chunk_right(later, chunk).start()
        chunk_left(s, c).wait_send()
        chunk_left(later, chunk).start()
        chunk_right(s, c).wait_recv()
        chunk_left(s, c).wait_recv()

    def relay_tissue(s):
        tis_right(s).wait_recv()
        tis_right(s + 1).start()
        tis_left(s).wait_recv()

        @pl.when(s < HALF - 1)
        def _():
            tis_left(s + 1).start()

        tis_right(s).wait_send()
        tis_left(s).wait_send()

    relay_tissue(1)

    def first_points(low, high):
        @pl.loop(low, high)
        def _(c):
            relay(1, c)
            own_units(2 * c, 2)

    first_points(0, HP - 3)
    q_up(0).wait_recv()
    q_on_up().start()
    q_down(1).wait_recv()
    q_on_down().start()
    first_points(HP - 3, HP)

    for dy in range(1, NY):
        tab_copy(dy).wait_recv()
    tabv[0] = tab[0]
    moves = [pltpu.make_async_copy(tabv, tabs, loc.at[3]), pltpu.make_async_copy(tab, tabo, loc.at[4])]
    for move in moves:
        move.start()
    for move in moves:
        move.wait()
    q_up(1).wait_recv()
    q_down(0).wait_recv()
    q_on_up().wait_recv()
    q_on_down().wait_recv()
    fill(work_o, 0)

    def find_places():
        @pl.loop(0, UNITS)
        def _(u):
            for j in range(SPAN):
                b = routes[j, u]
                dy = ((b >> 4) + NY - y) & (NY - 1)
                d = (z + NZ - (b & (NZ - 1))) & (NZ - 1)
                places[2 * (u * SPAN + j)] = dy * NZ + d
                places[2 * (u * SPAN + j) + 1] = (tabo[dy, 0, 2 * d] != u).astype(jnp.int32)

    @pl.loop(2, HALF + 1)
    def _(s):
        before_r, before_l = s - 1, NZ + 1 - s

        @pl.when(s < HALF)
        def _():
            relay_tissue(s)

        fill(work_r, before_r)
        fill(work_l, before_l)

        @pl.when(s == 3)
        def _():
            find_places()
            for dy in range(1, NY):
                tab_copy(dy).wait_send()
            for part in range(2):
                q_up(part).wait_send()
                q_down(part).wait_send()
            q_on_up().wait_send()
            q_on_down().wait_send()

        @pl.when(s == 4)
        def _():
            ret_wait(0)

        @pl.when(s >= 4)
        def _():
            ret_wait(s - 3)
            ret_wait(NZ + 3 - s)

        @pl.loop(0, NY)
        def _(dy):
            @pl.when(s < HALF)
            def _():
                relay(s, 2 * dy)
                relay(s, 2 * dy + 1)

            slots([(work, d, dy, c) for work, d in ((work_r, before_r), (work_l, before_l)) for c in range(2)])
            give_back(dy, before_r)
            give_back(dy, before_l)

            @pl.when(s == 2)
            def _():
                slots([(work_o, 0, dy, c) for c in range(2)])
                give_back(dy, 0)

    tis_right(HALF).wait_send()
    tis_right(HALF).wait_recv()
    for d in (HALF - 2, HALF + 2, HALF - 1, HALF + 1):
        ret_wait(d)

    for c in range(WINDOW):
        chunk_right(HALF, c).wait_recv()
        work_r[c] = kv[HALF, c]
        chunk_left(HALF, c).wait_recv()
        work_r[c + WINDOW] = kv[HALF, c + WINDOW]

    @pl.loop(0, NY // 2)
    def _(i):
        pair = [2 + i, 1 - i]
        slots([(work_r, HALF, dy, c) for dy in pair for c in range(2)])
        for dy in pair:
            give_back(dy, HALF)

    for c in range(WINDOW):
        chunk_right(HALF, c).wait_send()
        chunk_left(HALF, c).wait_send()
    ret_wait(HALF)

    mid = PAIR // 2

    def combine(u):
        tile, g = u // HP, u % HP
        spots = [(places[2 * (u * SPAN + j)], places[2 * (u * SPAN + j) + 1]) for j in range(SPAN)]
        stats = [ret_in[a, c, PAIR:ROWS, :].astype(jnp.float32) for a, c in spots]
        own = own_stat[u]
        rows = []
        for h in range(2):
            span = slice(h * mid, (h + 1) * mid)
            shifts = [st[h : h + 1, :] for st in stats]
            totals = [st[2 + h : 3 + h, :] for st in stats]
            top = own[h : h + 1, :]
            for sh in shifts:
                top = jnp.maximum(top, sh)
            own_w = jnp.exp(own[h : h + 1, :] - top)
            ws = [jnp.exp(sh - top) for sh in shifts]
            den = own_w * own[2 + h : 3 + h, :]
            for w, t in zip(ws, totals):
                den = den + w * t
            inv = 1.0 / den
            num = own_acc[u, span, :] * (own_w * inv)
            for (a, c), w in zip(spots, ws):
                num = num + ret_in[a, c, span, :].astype(jnp.float32) * (w * inv)
            rows.append(num)
        result = jnp.concatenate(rows, axis=0)
        rows_at = pl.ds(pl.multiple_of(tile * TILE, TILE), TILE)
        out[rows_at, pl.ds(pl.multiple_of(g * PAIR, PAIR), PAIR)] = result.T.astype(jnp.bfloat16)

    @pl.loop(0, UNITS // 4)
    def _(i):
        for k in range(4):
            combine(4 * i + k)


def local(queries, key_rows, values, tissue, routes):
    vmem = pl.BlockSpec(memory_space=pltpu.VMEM)
    hbm = pl.BlockSpec(memory_space=pltpu.HBM)
    dma = pltpu.SemaphoreType.DMA
    steps = HALF + 1
    rows = (2 * TILE, HP * PAIR)
    block = (HP, 4, PAIR, TILE)
    out = pl.pallas_call(
        kernel,
        out_shape=jax.ShapeDtypeStruct(rows, jnp.bfloat16),
        in_specs=[hbm] * 5,
        out_specs=vmem,
        scratch_shapes=[
            pltpu.SMEM((1, 2), jnp.int32),
            pltpu.SMEM((SPAN, UNITS), jnp.int32),
            pltpu.VMEM(rows, jnp.bfloat16),
            pltpu.VMEM(rows, jnp.bfloat16),
            pltpu.VMEM(rows, jnp.bfloat16),
            pltpu.VMEM((NZ,) + block, jnp.bfloat16),
            pltpu.VMEM((NZ, 2, 8, 128), jnp.int32),
            pltpu.VMEM(block, jnp.bfloat16),
            pltpu.VMEM(block, jnp.bfloat16),
            pltpu.VMEM(block, jnp.bfloat16),
            pltpu.VMEM((NY, UNITS, PAIR, TILE), jnp.bfloat16),
            pltpu.VMEM((NY, 8, 128), jnp.int32),
            pltpu.VMEM((NY, 8, 128), jnp.int32),
            pltpu.SMEM((NY, 8, 128), jnp.int32),
            pltpu.SMEM((NY, 8, 128), jnp.int32),
            pltpu.SMEM((2 * UNITS * SPAN,), jnp.int32),
            pltpu.VMEM((NY, NZ, 2, ROWS, TILE), jnp.bfloat16),
            pltpu.VMEM((NY * NZ, 2, ROWS, TILE), jnp.bfloat16),
            pltpu.VMEM((UNITS, PAIR, TILE), jnp.float32),
            pltpu.VMEM((UNITS, 8, 128), jnp.float32),
            dma((steps, HP)), dma((steps, HP)), dma((steps, HP)), dma((steps, HP)),
            dma((steps,)), dma((steps,)), dma((steps,)), dma((steps,)),
            dma((3, 2)), dma((3, 2)), dma((NY,)), dma((NY,)),
            dma((NY, NZ)), dma((NY, NZ)), dma((7,)),
        ],
        compiler_params=pltpu.CompilerParams(
            collective_id=0, has_side_effects=True, vmem_limit_bytes=53 * 1024 * 1024
        ),
    )(tissue, routes.transpose(0, 2, 1), queries, key_rows, values)
    return out[None]


def solution(mesh):
    placed = (
        P("slide", "seq", None),
        P("slide", "seq", None),
        P("slide", "seq", None),
        P("slide", "seq"),
        P("slide", "seq", None),
    )
    return jax.shard_map(
        local, mesh=mesh, in_specs=placed, out_specs=P("slide", "seq", None), check_vma=False
    )
```

```python
import jax
import jax.numpy as jnp
from jax import lax
from jax.experimental import pallas as pl
from jax.experimental.pallas import tpu as pltpu
from jax.sharding import PartitionSpec as P

NY = 4
NZ = 16
TILE = 128
HP = 8
PAIR = 128
HALF = NZ // 2
WINDOW = HP // 2
UNITS = 16
SPAN = 4
PIECE = 16
PIECES = PAIR // PIECE

big_negative = -1e30
MESH = pl.DeviceIdType.MESH


def halves(unit):
    mid = PAIR // 2
    zero = jnp.zeros((mid, TILE), unit.dtype)
    upper = jnp.concatenate([unit[:mid], zero], axis=1)
    return jnp.concatenate([upper, jnp.concatenate([zero, unit[mid:]], axis=1)], axis=0)


def fold(both):
    mid = PAIR // 2
    return jnp.concatenate([both[:mid, :TILE], both[mid:, TILE:]], axis=0)


def by_head(pair_row):
    return pair_row[:, :TILE], pair_row[:, TILE:]


def kernel(
    tissue_hbm, routes_hbm, q_hbm, k_hbm, v_hbm, out,
    tissue, routes, q_rows, k_rows, v_rows, kv, tis, work_o, work_r, work_l, qs, tab, tabv, tabs, tabo, places,
    ret_out, ret_in, own_acc, own_stat,
    rs, rr, ls, lr, trs, trr, tls, tlr, q_send, q_recv, t_send, t_recv, ret_s, ret_r, loc,
):
    me = lax.axis_index("seq")
    y, z = me // NZ, me % NZ

    loads = [
        pltpu.make_async_copy(k_hbm.at[0], k_rows, loc.at[0]),
        pltpu.make_async_copy(v_hbm.at[0], v_rows, loc.at[1]),
        pltpu.make_async_copy(q_hbm.at[0], q_rows, loc.at[2]),
        pltpu.make_async_copy(routes_hbm.at[0], routes, loc.at[5]),
        pltpu.make_async_copy(tissue_hbm, tissue, loc.at[6]),
    ]
    for load in loads:
        load.start()

    def at(row, column):
        return {"seq": row % NY * NZ + column % NZ}

    right, left = at(y, z + 1), at(y, z + NZ - 1)

    def peer(dy):
        return at(y + dy, z)

    def remote(src, dst, send, recv, device):
        return pltpu.make_async_remote_copy(
            src_ref=src, dst_ref=dst, send_sem=send, recv_sem=recv,
            device_id=device, device_id_type=MESH,
        )

    barrier = pltpu.get_barrier_semaphore()
    for device in [right, left] + [peer(dy) for dy in range(1, NY)]:
        pl.semaphore_signal(barrier, inc=1, device_id=device, device_id_type=MESH)

    def chunk_right(s, c):
        return remote(kv.at[s - 1, c], kv.at[s, c], rs.at[s, c], rr.at[s, c], right)

    def chunk_left(s, c):
        pair = (c + WINDOW) % HP
        return remote(
            kv.at[(NZ + 1 - s) % NZ, pair], kv.at[NZ - s, pair], ls.at[s, c], lr.at[s, c], left
        )

    def first_hop(c, pair, slot_at, send, recv, device):
        columns = pl.ds(pl.multiple_of(pair * PAIR, PAIR), PAIR)
        for i, src in enumerate((k_hbm, v_hbm)):
            for t in range(2):
                tokens = pl.ds(t * TILE, TILE)
                remote(
                    src.at[0, tokens, columns], kv.at[slot_at, pair, 2 * i + t],
                    send.at[1, c], recv.at[1, c], device,
                ).start()

    def start_first(c):
        first_hop(c, c, 1, rs, rr, right)
        first_hop(c, (c + WINDOW) % HP, NZ - 1, ls, lr, left)

    def tis_right(s):
        return remote(tis.at[s - 1], tis.at[s], trs.at[s], trr.at[s], right)

    def tis_left(s):
        return remote(tis.at[(NZ + 1 - s) % NZ], tis.at[NZ - s], tls.at[s], tlr.at[s], left)

    def tab_copy(dy):
        back = (NY - dy) % NY
        return remote(tab.at[dy], tabv.at[back], t_send.at[dy], t_recv.at[back], peer(dy))

    half = UNITS // 2

    def q_up(part):
        units = pl.ds(part * half, half)
        return remote(qs.at[0, units], qs.at[NY - 1, units], q_send.at[0, part], q_recv.at[0, part], peer(1))

    def q_down(part):
        units = pl.ds(part * half, half)
        return remote(qs.at[0, units], qs.at[1, units], q_send.at[1, part], q_recv.at[1, part], peer(NY - 1))

    def q_on_up():
        units = pl.ds(0, half)
        return remote(qs.at[NY - 1, units], qs.at[2, units], q_send.at[2, 0], q_recv.at[2, 0], peer(1))

    def q_on_down():
        units = pl.ds(half, half)
        return remote(qs.at[1, units], qs.at[2, units], q_send.at[2, 1], q_recv.at[2, 1], peer(NY - 1))

    def lay_pair(g):
        columns = slice(g * PAIR, (g + 1) * PAIR)
        for t in range(2):
            tokens = slice(t * TILE, (t + 1) * TILE)
            work_o[g, t] = k_rows[tokens, columns]
            work_o[g, 2 + t] = v_rows[tokens, columns].T

    pl.semaphore_wait(barrier, 2 + NY - 1)
    for c in range(WINDOW):
        start_first(c)

    for load in loads[3:]:
        load.wait()
    for t in range(2):
        tis[0, t] = jnp.full((8, 128), (tissue[0, t] == 1).astype(jnp.int32), jnp.int32)
    tis_right(1).start()
    tis_left(1).start()

    lane = lax.broadcasted_iota(jnp.int32, (8, 128), 1)
    row = lax.broadcasted_iota(jnp.int32, (8, 128), 0)
    block = (y + row) % NY * NZ + (z + NZ - (lane // 2) % NZ) % NZ
    first = jnp.full((8, 128), UNITS - 1, jnp.int32)
    last = jnp.zeros((8, 128), jnp.int32)
    for u in range(UNITS):
        named = block == routes[0, u]
        for j in range(1, SPAN):
            named = named | (block == routes[j, u])
        first = jnp.where(named, jnp.minimum(first, u), first)
        last = jnp.where(named, u, last)
    table = jnp.where(lane % 2 == 0, first, last)
    for dy in range(NY):
        tab[dy] = jnp.broadcast_to(table[dy : dy + 1], (8, 128))
    for dy in range(1, NY):
        tab_copy(dy).start()

    scale = jnp.bfloat16((PAIR // 2) ** -0.5)
    loads[2].wait()

    def lay_queries(part):
        for i in range(half):
            u = part * half + i
            tile, g = u // HP, u % HP
            qs[0, u] = (q_rows[tile * TILE : (tile + 1) * TILE, g * PAIR : (g + 1) * PAIR] * scale).T

    lay_queries(0)
    q_up(0).start()
    lay_queries(1)
    q_down(1).start()
    q_up(1).start()
    q_down(0).start()

    loads[0].wait()
    loads[1].wait()
    for g in range(HP):
        lay_pair(g)

    def own_units(low, count):
        numbers = [low + i for i in range(count)]

        def scores_of(u):
            return jnp.dot(
                work_o[u % HP, u // HP], halves(qs[0, u]), preferred_element_type=jnp.float32
            )

        scores = scores_of(numbers[0])
        done = []
        for i, u in enumerate(numbers):
            later = scores_of(numbers[i + 1]) if i + 1 < count else None
            shift = jnp.max(scores, axis=0, keepdims=True)
            probs = jnp.exp(scores - shift)
            total = jnp.sum(probs, axis=0, keepdims=True)
            both = jnp.dot(
                work_o[u % HP, 2 + u // HP], probs.astype(jnp.bfloat16), preferred_element_type=jnp.float32
            )
            done.append((u, fold(both), by_head(shift) + by_head(total)))
            scores = later
        for u, folded, four in done:
            own_acc[u] = folded
            own_stat[u] = jnp.concatenate(four + four, axis=0)

    def slots(jobs):
        def scores_of(job):
            work, d, dy, c = job
            u = tabs[dy, 0, d * 2 + c]
            g = u & (HP - 1)
            unit = halves(qs[dy, u])
            keep = []
            for t in range(2):
                row = tis[d, t, 0:1, :]
                if work is work_o:
                    row = row * (1 - ((dy == 0) & ((u >> 3) == t)).astype(jnp.int32))
                keep.append(jnp.concatenate([row, row], axis=1) != 0)
            value = jnp.concatenate([work[g, 2], work[g, 3]], axis=1)
            keys = jnp.concatenate([work[g, 0], work[g, 1]], axis=0)
            both = jnp.dot(keys, unit, preferred_element_type=jnp.float32)
            return [both[:TILE], both[TILE:]], keep, value

        ready = scores_of(jobs[0])
        done = []
        for i, job in enumerate(jobs):
            later = scores_of(jobs[i + 1]) if i + 1 < len(jobs) else None
            scores, keep, value = ready
            peaks = [
                jnp.where(keep[t], jnp.max(scores[t], axis=0, keepdims=True), big_negative)
                for t in range(2)
            ]
            shift = jnp.maximum(peaks[0], peaks[1]).astype(jnp.bfloat16).astype(jnp.float32)
            weights = [
                jnp.exp(scores[t] - jnp.where(keep[t], shift, -big_negative)) for t in range(2)
            ]
            total = jnp.sum(weights[0], axis=0, keepdims=True) + jnp.sum(weights[1], axis=0, keepdims=True)
            both = jnp.dot(
                value,
                jnp.concatenate([w.astype(jnp.bfloat16) for w in weights], axis=0),
                preferred_element_type=jnp.float32,
            )
            four = by_head(shift) + by_head(total)
            done.append((job, fold(both), jnp.concatenate(four * 2, axis=0)))
            ready = later
        for i, ((work, d, dy, c), folded, stat) in enumerate(done):
            pieces = folded.astype(jnp.bfloat16).reshape(PIECES, PIECE, TILE)
            ret_out[dy, d, c * PIECES : (c + 1) * PIECES] = pieces
            if c == 1:
                both = jnp.concatenate([done[i - 1][2], stat], axis=0)
                ret_out[dy, d, 2 * PIECES] = both.astype(jnp.bfloat16)

    def ret_copy(dy, d):
        back = (NY - dy) % NY
        return remote(
            ret_out.at[dy, d], ret_in.at[back * NZ + d], ret_s.at[dy, d], ret_r.at[back, d], peer(dy)
        )

    def ret_local(d):
        return pltpu.make_async_copy(ret_out.at[0, d], ret_in.at[d], ret_r.at[0, d])

    def give_back(dy, d):
        @pl.when(dy == 0)
        def _():
            ret_local(d).start()

        @pl.when(dy > 0)
        def _():
            ret_copy(dy, d).start()

    def ret_wait(d):
        ret_local(d).wait()
        for dy in range(1, NY):
            ret_copy(dy, d).wait_send()
            ret_copy(dy, d).wait_recv()

    def fill_pair(work, d, g):
        for t in range(2):
            work[g, t] = kv[d, g, t]
            work[g, 2 + t] = kv[d, g, 2 + t].T

    def fill(work, d):
        for g in range(HP):
            fill_pair(work, d, g)

    def relay(s, c):
        later, chunk = s + (c + WINDOW) // HP, (c + WINDOW) % HP
        chunk_right(s, c).wait_send()
        chunk_left(s, c).wait_send()

        @pl.when(later == 1)
        def _():
            start_first(chunk)

        @pl.when(later > 1)
        def _():
            chunk_right(later, chunk).start()
            chunk_left(later, chunk).start()

        chunk_right(s, c).wait_recv()
        chunk_left(s, c).wait_recv()

    def relay_tissue(s):
        tis_right(s).wait_recv()
        tis_right(s + 1).start()
        tis_left(s).wait_recv()

        @pl.when(s < HALF - 1)
        def _():
            tis_left(s + 1).start()

        tis_right(s).wait_send()
        tis_left(s).wait_send()

    relay_tissue(1)

    def first_points(low, high):
        @pl.loop(low, high)
        def _(c):
            relay(1, c)
            own_units(2 * c, 2)

    first_points(0, HP - 3)
    q_up(0).wait_recv()
    q_on_up().start()
    q_down(1).wait_recv()
    q_on_down().start()
    first_points(HP - 3, HP)

    for dy in range(1, NY):
        tab_copy(dy).wait_recv()
    tabv[0] = tab[0]
    moves = [pltpu.make_async_copy(tabv, tabs, loc.at[3]), pltpu.make_async_copy(tab, tabo, loc.at[4])]
    for move in moves:
        move.start()
    for move in moves:
        move.wait()
    q_up(1).wait_recv()
    q_down(0).wait_recv()
    q_on_up().wait_recv()
    q_on_down().wait_recv()

    def find_places():
        @pl.loop(0, UNITS)
        def _(u):
            for j in range(SPAN):
                b = routes[j, u]
                dy = ((b >> 4) + NY - y) & (NY - 1)
                d = (z + NZ - (b & (NZ - 1))) & (NZ - 1)
                places[2 * (u * SPAN + j)] = dy * NZ + d
                places[2 * (u * SPAN + j) + 1] = (tabo[dy, 0, 2 * d] != u).astype(jnp.int32)

    @pl.loop(2, HALF + 1)
    def _(s):
        before_r, before_l = s - 1, NZ + 1 - s

        @pl.when(s < HALF)
        def _():
            relay_tissue(s)

        fill(work_r, before_r)
        fill(work_l, before_l)

        @pl.when(s == 3)
        def _():
            find_places()
            for dy in range(1, NY):
                tab_copy(dy).wait_send()
            for part in range(2):
                q_up(part).wait_send()
                q_down(part).wait_send()
            q_on_up().wait_send()
            q_on_down().wait_send()

        @pl.when(s == 4)
        def _():
            ret_wait(0)

        @pl.when(s >= 4)
        def _():
            ret_wait(s - 3)
            ret_wait(NZ + 3 - s)

        @pl.loop(0, NY)
        def _(dy):
            @pl.when(s < HALF)
            def _():
                relay(s, 2 * dy)
                relay(s, 2 * dy + 1)

            slots([(work, d, dy, c) for work, d in ((work_r, before_r), (work_l, before_l)) for c in range(2)])
            give_back(dy, before_r)
            give_back(dy, before_l)

            @pl.when(s == 2)
            def _():
                slots([(work_o, 0, dy, c) for c in range(2)])
                give_back(dy, 0)

    tis_right(HALF).wait_send()
    tis_right(HALF).wait_recv()
    for d in (HALF - 2, HALF + 2, HALF - 1, HALF + 1):
        ret_wait(d)

    for c in range(WINDOW):
        chunk_right(HALF, c).wait_recv()
        fill_pair(work_r, HALF, c)
        chunk_left(HALF, c).wait_recv()
        fill_pair(work_r, HALF, c + WINDOW)

    @pl.loop(0, NY // 2)
    def _(i):
        pair = [2 + i, 1 - i]
        slots([(work_r, HALF, dy, c) for dy in pair for c in range(2)])
        for dy in pair:
            give_back(dy, HALF)

    for c in range(WINDOW):
        chunk_right(HALF, c).wait_send()
        chunk_left(HALF, c).wait_send()
    ret_wait(HALF)

    mid = PAIR // 2

    def combine(u):
        tile, g = u // HP, u % HP
        spots = [(places[2 * (u * SPAN + j)], places[2 * (u * SPAN + j) + 1]) for j in range(SPAN)]
        stats = []
        for a, c in spots:
            both = ret_in[a, 2 * PIECES].astype(jnp.float32)
            stats.append(jnp.where(c == 0, both[0:8], both[8:16]))
        own = own_stat[u]
        rows = []
        for h in range(2):
            span = slice(h * mid, (h + 1) * mid)
            shifts = [st[h : h + 1, :] for st in stats]
            totals = [st[2 + h : 3 + h, :] for st in stats]
            top = own[h : h + 1, :]
            for sh in shifts:
                top = jnp.maximum(top, sh)
            own_w = jnp.exp(own[h : h + 1, :] - top)
            ws = [jnp.exp(sh - top) for sh in shifts]
            den = own_w * own[2 + h : 3 + h, :]
            for w, t in zip(ws, totals):
                den = den + w * t
            inv = 1.0 / den
            num = own_acc[u, span, :] * (own_w * inv)
            for (a, c), w in zip(spots, ws):
                first = c * PIECES + h * (PIECES // 2)
                part = jnp.concatenate([ret_in[a, first + i] for i in range(PIECES // 2)], axis=0)
                num = num + part.astype(jnp.float32) * (w * inv)
            rows.append(num)
        result = jnp.concatenate(rows, axis=0)
        rows_at = pl.ds(pl.multiple_of(tile * TILE, TILE), TILE)
        out[rows_at, pl.ds(pl.multiple_of(g * PAIR, PAIR), PAIR)] = result.T.astype(jnp.bfloat16)

    @pl.loop(0, UNITS // 4)
    def _(i):
        for k in range(4):
            combine(4 * i + k)


def local(queries, key_rows, values, tissue, routes):
    vmem = pl.BlockSpec(memory_space=pltpu.VMEM)
    hbm = pl.BlockSpec(memory_space=pltpu.HBM)
    dma = pltpu.SemaphoreType.DMA
    steps = HALF + 1
    rows = (2 * TILE, HP * PAIR)
    block = (HP, 4, PAIR, TILE)
    out = pl.pallas_call(
        kernel,
        out_shape=jax.ShapeDtypeStruct(rows, jnp.bfloat16),
        in_specs=[hbm] * 5,
        out_specs=vmem,
        scratch_shapes=[
            pltpu.SMEM((1, 2), jnp.int32),
            pltpu.SMEM((SPAN, UNITS), jnp.int32),
            pltpu.VMEM(rows, jnp.bfloat16),
            pltpu.VMEM(rows, jnp.bfloat16),
            pltpu.VMEM(rows, jnp.bfloat16),
            pltpu.VMEM((NZ,) + block, jnp.bfloat16),
            pltpu.VMEM((NZ, 2, 8, 128), jnp.int32),
            pltpu.VMEM(block, jnp.bfloat16),
            pltpu.VMEM(block, jnp.bfloat16),
            pltpu.VMEM(block, jnp.bfloat16),
            pltpu.VMEM((NY, UNITS, PAIR, TILE), jnp.bfloat16),
            pltpu.VMEM((NY, 8, 128), jnp.int32),
            pltpu.VMEM((NY, 8, 128), jnp.int32),
            pltpu.SMEM((NY, 8, 128), jnp.int32),
            pltpu.SMEM((NY, 8, 128), jnp.int32),
            pltpu.SMEM((2 * UNITS * SPAN,), jnp.int32),
            pltpu.VMEM((NY, NZ, 2 * PIECES + 1, PIECE, TILE), jnp.bfloat16),
            pltpu.VMEM((NY * NZ, 2 * PIECES + 1, PIECE, TILE), jnp.bfloat16),
            pltpu.VMEM((UNITS, PAIR, TILE), jnp.float32),
            pltpu.VMEM((UNITS, 8, 128), jnp.float32),
            dma((steps, HP)), dma((steps, HP)), dma((steps, HP)), dma((steps, HP)),
            dma((steps,)), dma((steps,)), dma((steps,)), dma((steps,)),
            dma((3, 2)), dma((3, 2)), dma((NY,)), dma((NY,)),
            dma((NY, NZ)), dma((NY, NZ)), dma((7,)),
        ],
        compiler_params=pltpu.CompilerParams(
            collective_id=0, has_side_effects=True, vmem_limit_bytes=53 * 1024 * 1024
        ),
    )(tissue, routes.transpose(0, 2, 1), queries, key_rows, values)
    return out[None]


def solution(mesh):
    placed = (
        P("slide", "seq", None),
        P("slide", "seq", None),
        P("slide", "seq", None),
        P("slide", "seq"),
        P("slide", "seq", None),
    )
    return jax.shard_map(
        local, mesh=mesh, in_specs=placed, out_specs=P("slide", "seq", None), check_vma=False
    )
```

```python
import jax
import jax.numpy as jnp
from jax import lax
from jax.experimental import pallas as pl
from jax.experimental.pallas import tpu as pltpu
from jax.sharding import PartitionSpec as P

NY = 4
NZ = 16
TILE = 128
HP = 8
PAIR = 128
HALF = NZ // 2
WINDOW = HP // 2
UNITS = 16
SPAN = 4
PIECE = 16
PIECES = PAIR // PIECE

big_negative = -1e30
MESH = pl.DeviceIdType.MESH


def halves(unit):
    mid = PAIR // 2
    zero = jnp.zeros((mid, TILE), unit.dtype)
    upper = jnp.concatenate([unit[:mid], zero], axis=1)
    return jnp.concatenate([upper, jnp.concatenate([zero, unit[mid:]], axis=1)], axis=0)


def fold(both):
    mid = PAIR // 2
    return jnp.concatenate([both[:mid, :TILE], both[mid:, TILE:]], axis=0)


def by_head(pair_row):
    return pair_row[:, :TILE], pair_row[:, TILE:]


def kernel(
    small_hbm, q_hbm, k_hbm, v_hbm, out,
    routes, q_rows, k_rows, v_rows, kv, tis, work_o, work_r, work_l, qs, tab, tabv, tabs, tabo, places,
    ret_out, ret_in, own_acc, own_stat,
    rs, rr, ls, lr, trs, trr, tls, tlr, q_send, q_recv, t_send, t_recv, ret_s, ret_r, loc,
):
    me = lax.axis_index("seq")
    y, z = me // NZ, me % NZ

    loads = [
        pltpu.make_async_copy(k_hbm.at[0], k_rows, loc.at[0]),
        pltpu.make_async_copy(v_hbm.at[0], v_rows, loc.at[1]),
        pltpu.make_async_copy(q_hbm.at[0], q_rows, loc.at[2]),
        pltpu.make_async_copy(small_hbm.at[0], routes, loc.at[5]),
    ]
    for load in loads:
        load.start()

    def at(row, column):
        return {"seq": row % NY * NZ + column % NZ}

    right, left = at(y, z + 1), at(y, z + NZ - 1)

    def peer(dy):
        return at(y + dy, z)

    def remote(src, dst, send, recv, device):
        return pltpu.make_async_remote_copy(
            src_ref=src, dst_ref=dst, send_sem=send, recv_sem=recv,
            device_id=device, device_id_type=MESH,
        )

    barrier = pltpu.get_barrier_semaphore()
    for device in [right, left] + [peer(dy) for dy in range(1, NY)]:
        pl.semaphore_signal(barrier, inc=1, device_id=device, device_id_type=MESH)

    def chunk_right(s, c):
        return remote(kv.at[s - 1, c], kv.at[s, c], rs.at[s, c], rr.at[s, c], right)

    def chunk_left(s, c):
        pair = (c + WINDOW) % HP
        return remote(
            kv.at[(NZ + 1 - s) % NZ, pair], kv.at[NZ - s, pair], ls.at[s, c], lr.at[s, c], left
        )

    def tis_right(s):
        return remote(tis.at[s - 1], tis.at[s], trs.at[s], trr.at[s], right)

    def tis_left(s):
        return remote(tis.at[(NZ + 1 - s) % NZ], tis.at[NZ - s], tls.at[s], tlr.at[s], left)

    def tab_copy(dy):
        back = (NY - dy) % NY
        return remote(tab.at[dy], tabv.at[back], t_send.at[dy], t_recv.at[back], peer(dy))

    half = UNITS // 2

    def q_up(part):
        units = pl.ds(part * half, half)
        return remote(qs.at[0, units], qs.at[NY - 1, units], q_send.at[0, part], q_recv.at[0, part], peer(1))

    def q_down(part):
        units = pl.ds(part * half, half)
        return remote(qs.at[0, units], qs.at[1, units], q_send.at[1, part], q_recv.at[1, part], peer(NY - 1))

    def q_on_up():
        units = pl.ds(0, half)
        return remote(qs.at[NY - 1, units], qs.at[2, units], q_send.at[2, 0], q_recv.at[2, 0], peer(1))

    def q_on_down():
        units = pl.ds(half, half)
        return remote(qs.at[1, units], qs.at[2, units], q_send.at[2, 1], q_recv.at[2, 1], peer(NY - 1))

    def lay_pair(g):
        columns = slice(g * PAIR, (g + 1) * PAIR)
        for t in range(2):
            tokens = slice(t * TILE, (t + 1) * TILE)
            kv[0, g, t] = k_rows[tokens, columns]
            kv[0, g, 2 + t] = v_rows[tokens, columns].T

    loads[0].wait()
    loads[1].wait()
    for c in range(WINDOW):
        lay_pair(c)
        lay_pair(c + WINDOW)
        if c == 0:
            pl.semaphore_wait(barrier, 2 + NY - 1)
        chunk_right(1, c).start()
        chunk_left(1, c).start()

    for load in loads[3:]:
        load.wait()
    for t in range(2):
        tis[0, t] = jnp.full((8, 128), (routes[SPAN, t] == 1).astype(jnp.int32), jnp.int32)
    tis_right(1).start()
    tis_left(1).start()

    lane = lax.broadcasted_iota(jnp.int32, (8, 128), 1)
    row = lax.broadcasted_iota(jnp.int32, (8, 128), 0)
    block = (y + row) % NY * NZ + (z + NZ - (lane // 2) % NZ) % NZ
    first = jnp.full((8, 128), UNITS - 1, jnp.int32)
    last = jnp.zeros((8, 128), jnp.int32)
    for u in range(UNITS):
        named = block == routes[0, u]
        for j in range(1, SPAN):
            named = named | (block == routes[j, u])
        first = jnp.where(named, jnp.minimum(first, u), first)
        last = jnp.where(named, u, last)
    table = jnp.where(lane % 2 == 0, first, last)
    for dy in range(NY):
        tab[dy] = jnp.broadcast_to(table[dy : dy + 1], (8, 128))
    for dy in range(1, NY):
        tab_copy(dy).start()

    scale = jnp.bfloat16((PAIR // 2) ** -0.5)
    loads[2].wait()

    def lay_queries(part):
        for i in range(half):
            u = part * half + i
            tile, g = u // HP, u % HP
            qs[0, u] = (q_rows[tile * TILE : (tile + 1) * TILE, g * PAIR : (g + 1) * PAIR] * scale).T

    lay_queries(0)
    q_up(0).start()
    lay_queries(1)
    q_down(1).start()
    q_up(1).start()
    q_down(0).start()

    def own_units(low, count):
        numbers = [low + i for i in range(count)]

        def scores_of(u):
            return jnp.dot(
                kv[0, u % HP, u // HP], halves(qs[0, u]), preferred_element_type=jnp.float32
            )

        scores = scores_of(numbers[0])
        done = []
        for i, u in enumerate(numbers):
            later = scores_of(numbers[i + 1]) if i + 1 < count else None
            shift = jnp.max(scores, axis=0, keepdims=True)
            probs = jnp.exp(scores - shift)
            total = jnp.sum(probs, axis=0, keepdims=True)
            both = jnp.dot(
                kv[0, u % HP, 2 + u // HP], probs.astype(jnp.bfloat16), preferred_element_type=jnp.float32
            )
            done.append((u, fold(both), by_head(shift) + by_head(total)))
            scores = later
        for u, folded, four in done:
            own_acc[u] = folded
            own_stat[u] = jnp.concatenate(four + four, axis=0)

    def slots(jobs):
        def scores_of(job):
            work, d, dy, c = job
            u = tabs[dy, 0, d * 2 + c]
            g = u & (HP - 1)
            unit = halves(qs[dy, u])
            keep = []
            for t in range(2):
                row = tis[d, t, 0:1, :]
                if work is work_o:
                    row = row * (1 - ((dy == 0) & ((u >> 3) == t)).astype(jnp.int32))
                keep.append(jnp.concatenate([row, row], axis=1) != 0)
            value = jnp.concatenate([work[g, 2], work[g, 3]], axis=1)
            keys = jnp.concatenate([work[g, 0], work[g, 1]], axis=0)
            both = jnp.dot(keys, unit, preferred_element_type=jnp.float32)
            return [both[:TILE], both[TILE:]], keep, value

        ready = scores_of(jobs[0])
        done = []
        for i, job in enumerate(jobs):
            later = scores_of(jobs[i + 1]) if i + 1 < len(jobs) else None
            scores, keep, value = ready
            peaks = [
                jnp.where(keep[t], jnp.max(scores[t], axis=0, keepdims=True), big_negative)
                for t in range(2)
            ]
            shift = jnp.maximum(peaks[0], peaks[1]).astype(jnp.bfloat16).astype(jnp.float32)
            weights = [
                jnp.exp(scores[t] - jnp.where(keep[t], shift, -big_negative)) for t in range(2)
            ]
            total = jnp.sum(weights[0], axis=0, keepdims=True) + jnp.sum(weights[1], axis=0, keepdims=True)
            both = jnp.dot(
                value,
                jnp.concatenate([w.astype(jnp.bfloat16) for w in weights], axis=0),
                preferred_element_type=jnp.float32,
            )
            four = by_head(shift) + by_head(total)
            done.append((job, fold(both), jnp.concatenate(four * 2, axis=0)))
            ready = later
        for i, ((work, d, dy, c), folded, stat) in enumerate(done):
            pieces = folded.astype(jnp.bfloat16).reshape(PIECES, PIECE, TILE)
            ret_out[dy, d, c * PIECES : (c + 1) * PIECES] = pieces
            if c == 1:
                both = jnp.concatenate([done[i - 1][2], stat], axis=0)
                ret_out[dy, d, 2 * PIECES] = both.astype(jnp.bfloat16)

    def ret_copy(dy, d):
        back = (NY - dy) % NY
        return remote(
            ret_out.at[dy, d], ret_in.at[back * NZ + d], ret_s.at[dy, d], ret_r.at[back, d], peer(dy)
        )

    def ret_local(d):
        return pltpu.make_async_copy(ret_out.at[0, d], ret_in.at[d], ret_r.at[0, d])

    def give_back(dy, d):
        @pl.when(dy == 0)
        def _():
            ret_local(d).start()

        @pl.when(dy > 0)
        def _():
            ret_copy(dy, d).start()

    def ret_wait(d):
        ret_local(d).wait()
        for dy in range(1, NY):
            ret_copy(dy, d).wait_send()
            ret_copy(dy, d).wait_recv()

    def fill(work, d):
        for g in range(HP):
            work[g] = kv[d, g]

    def relay(s, c):
        later, chunk = s + (c + WINDOW) // HP, (c + WINDOW) % HP
        chunk_right(s, c).wait_send()
        chunk_right(later, chunk).start()
        chunk_left(s, c).wait_send()
        chunk_left(later, chunk).start()
        chunk_right(s, c).wait_recv()
        chunk_left(s, c).wait_recv()

    def relay_tissue(s):
        tis_right(s).wait_recv()
        tis_right(s + 1).start()
        tis_left(s).wait_recv()

        @pl.when(s < HALF - 1)
        def _():
            tis_left(s + 1).start()

        tis_right(s).wait_send()
        tis_left(s).wait_send()

    relay_tissue(1)

    def first_points(low, high):
        @pl.loop(low, high)
        def _(c):
            relay(1, c)
            own_units(2 * c, 2)

    first_points(0, HP - 3)
    q_up(0).wait_recv()
    q_on_up().start()
    q_down(1).wait_recv()
    q_on_down().start()
    first_points(HP - 3, HP)

    for dy in range(1, NY):
        tab_copy(dy).wait_recv()
    tabv[0] = tab[0]
    moves = [pltpu.make_async_copy(tabv, tabs, loc.at[3]), pltpu.make_async_copy(tab, tabo, loc.at[4])]
    for move in moves:
        move.start()
    for move in moves:
        move.wait()
    q_up(1).wait_recv()
    q_down(0).wait_recv()
    q_on_up().wait_recv()
    q_on_down().wait_recv()
    fill(work_o, 0)

    def find_places():
        @pl.loop(0, UNITS)
        def _(u):
            for j in range(SPAN):
                b = routes[j, u]
                dy = ((b >> 4) + NY - y) & (NY - 1)
                d = (z + NZ - (b & (NZ - 1))) & (NZ - 1)
                places[2 * (u * SPAN + j)] = dy * NZ + d
                places[2 * (u * SPAN + j) + 1] = (tabo[dy, 0, 2 * d] != u).astype(jnp.int32)

    @pl.loop(2, HALF + 1)
    def _(s):
        before_r, before_l = s - 1, NZ + 1 - s

        @pl.when(s < HALF)
        def _():
            relay_tissue(s)

        fill(work_r, before_r)
        fill(work_l, before_l)

        @pl.when(s == 3)
        def _():
            find_places()
            for dy in range(1, NY):
                tab_copy(dy).wait_send()
            for part in range(2):
                q_up(part).wait_send()
                q_down(part).wait_send()
            q_on_up().wait_send()
            q_on_down().wait_send()

        @pl.when(s == 4)
        def _():
            ret_wait(0)

        @pl.when(s >= 4)
        def _():
            ret_wait(s - 3)
            ret_wait(NZ + 3 - s)

        @pl.loop(0, NY)
        def _(dy):
            @pl.when(s < HALF)
            def _():
                relay(s, 2 * dy)
                relay(s, 2 * dy + 1)

            slots([(work, d, dy, c) for work, d in ((work_r, before_r), (work_l, before_l)) for c in range(2)])
            give_back(dy, before_r)
            give_back(dy, before_l)

            @pl.when(s == 2)
            def _():
                slots([(work_o, 0, dy, c) for c in range(2)])
                give_back(dy, 0)

    tis_right(HALF).wait_send()
    tis_right(HALF).wait_recv()
    for d in (HALF - 2, HALF + 2, HALF - 1, HALF + 1):
        ret_wait(d)

    for c in range(WINDOW):
        chunk_right(HALF, c).wait_recv()
        work_r[c] = kv[HALF, c]
        chunk_left(HALF, c).wait_recv()
        work_r[c + WINDOW] = kv[HALF, c + WINDOW]

    @pl.loop(0, NY // 2)
    def _(i):
        pair = [2 + i, 1 - i]
        slots([(work_r, HALF, dy, c) for dy in pair for c in range(2)])
        for dy in pair:
            give_back(dy, HALF)

    for c in range(WINDOW):
        chunk_right(HALF, c).wait_send()
        chunk_left(HALF, c).wait_send()
    ret_wait(HALF)

    mid = PAIR // 2

    def combine(u):
        tile, g = u // HP, u % HP
        spots = [(places[2 * (u * SPAN + j)], places[2 * (u * SPAN + j) + 1]) for j in range(SPAN)]
        stats = []
        for a, c in spots:
            both = ret_in[a, 2 * PIECES].astype(jnp.float32)
            stats.append(jnp.where(c == 0, both[0:8], both[8:16]))
        own = own_stat[u]
        rows = []
        for h in range(2):
            span = slice(h * mid, (h + 1) * mid)
            shifts = [st[h : h + 1, :] for st in stats]
            totals = [st[2 + h : 3 + h, :] for st in stats]
            top = own[h : h + 1, :]
            for sh in shifts:
                top = jnp.maximum(top, sh)
            own_w = jnp.exp(own[h : h + 1, :] - top)
            ws = [jnp.exp(sh - top) for sh in shifts]
            den = own_w * own[2 + h : 3 + h, :]
            for w, t in zip(ws, totals):
                den = den + w * t
            inv = 1.0 / den
            num = own_acc[u, span, :] * (own_w * inv)
            for (a, c), w in zip(spots, ws):
                first = c * PIECES + h * (PIECES // 2)
                part = jnp.concatenate([ret_in[a, first + i] for i in range(PIECES // 2)], axis=0)
                num = num + part.astype(jnp.float32) * (w * inv)
            rows.append(num)
        result = jnp.concatenate(rows, axis=0)
        rows_at = pl.ds(pl.multiple_of(tile * TILE, TILE), TILE)
        out[rows_at, pl.ds(pl.multiple_of(g * PAIR, PAIR), PAIR)] = result.T.astype(jnp.bfloat16)

    @pl.loop(0, UNITS // 4)
    def _(i):
        for k in range(4):
            combine(4 * i + k)


def local(queries, key_rows, values, tissue, routes):
    wide = jnp.pad(tissue[:, None], ((0, 0), (0, 0), (0, UNITS - tissue.shape[1])))
    small = jnp.concatenate([routes.transpose(0, 2, 1), wide], axis=1)
    vmem = pl.BlockSpec(memory_space=pltpu.VMEM)
    hbm = pl.BlockSpec(memory_space=pltpu.HBM)
    dma = pltpu.SemaphoreType.DMA
    steps = HALF + 1
    rows = (2 * TILE, HP * PAIR)
    block = (HP, 4, PAIR, TILE)
    out = pl.pallas_call(
        kernel,
        out_shape=jax.ShapeDtypeStruct(rows, jnp.bfloat16),
        in_specs=[hbm] * 4,
        out_specs=vmem,
        scratch_shapes=[
            pltpu.SMEM((SPAN + 1, UNITS), jnp.int32),
            pltpu.VMEM(rows, jnp.bfloat16),
            pltpu.VMEM(rows, jnp.bfloat16),
            pltpu.VMEM(rows, jnp.bfloat16),
            pltpu.VMEM((NZ,) + block, jnp.bfloat16),
            pltpu.VMEM((NZ, 2, 8, 128), jnp.int32),
            pltpu.VMEM(block, jnp.bfloat16),
            pltpu.VMEM(block, jnp.bfloat16),
            pltpu.VMEM(block, jnp.bfloat16),
            pltpu.VMEM((NY, UNITS, PAIR, TILE), jnp.bfloat16),
            pltpu.VMEM((NY, 8, 128), jnp.int32),
            pltpu.VMEM((NY, 8, 128), jnp.int32),
            pltpu.SMEM((NY, 8, 128), jnp.int32),
            pltpu.SMEM((NY, 8, 128), jnp.int32),
            pltpu.SMEM((2 * UNITS * SPAN,), jnp.int32),
            pltpu.VMEM((NY, NZ, 2 * PIECES + 1, PIECE, TILE), jnp.bfloat16),
            pltpu.VMEM((NY * NZ, 2 * PIECES + 1, PIECE, TILE), jnp.bfloat16),
            pltpu.VMEM((UNITS, PAIR, TILE), jnp.float32),
            pltpu.VMEM((UNITS, 8, 128), jnp.float32),
            dma((steps, HP)), dma((steps, HP)), dma((steps, HP)), dma((steps, HP)),
            dma((steps,)), dma((steps,)), dma((steps,)), dma((steps,)),
            dma((3, 2)), dma((3, 2)), dma((NY,)), dma((NY,)),
            dma((NY, NZ)), dma((NY, NZ)), dma((6,)),
        ],
        compiler_params=pltpu.CompilerParams(
            collective_id=0, has_side_effects=True, vmem_limit_bytes=53 * 1024 * 1024
        ),
    )(small, queries, key_rows, values)
    return out[None]


def solution(mesh):
    placed = (
        P("slide", "seq", None),
        P("slide", "seq", None),
        P("slide", "seq", None),
        P("slide", "seq"),
        P("slide", "seq", None),
    )
    return jax.shard_map(
        local, mesh=mesh, in_specs=placed, out_specs=P("slide", "seq", None), check_vma=False
    )
```

```python
import jax
import jax.numpy as jnp
from jax import lax
from jax.experimental import pallas as pl
from jax.experimental.pallas import tpu as pltpu
from jax.sharding import PartitionSpec as P

NY = 4
NZ = 16
TILE = 128
HP = 8
PAIR = 128
HALF = NZ // 2
SPLIT = HP // 2
AHEAD = 6
UNITS = 16
SPAN = 4
PIECE = 16
PIECES = PAIR // PIECE

big_negative = -1e30
MESH = pl.DeviceIdType.MESH


def halves(unit):
    mid = PAIR // 2
    zero = jnp.zeros((mid, TILE), unit.dtype)
    upper = jnp.concatenate([unit[:mid], zero], axis=1)
    return jnp.concatenate([upper, jnp.concatenate([zero, unit[mid:]], axis=1)], axis=0)


def fold(both):
    mid = PAIR // 2
    return jnp.concatenate([both[:mid, :TILE], both[mid:, TILE:]], axis=0)


def by_head(pair_row):
    return pair_row[:, :TILE], pair_row[:, TILE:]


def kernel(
    small_hbm, q_hbm, k_hbm, v_hbm, out,
    routes, q_rows, k_rows, v_rows, kv, tis, work_o, work_r, work_l, qs, tab, tabv, tabs, tabo, places,
    ret_out, ret_in, own_acc, own_stat,
    rs, rr, ls, lr, trs, trr, tls, tlr, q_send, q_recv, t_send, t_recv, ret_s, ret_r, loc,
):
    me = lax.axis_index("seq")
    y, z = me // NZ, me % NZ

    loads = [
        pltpu.make_async_copy(k_hbm.at[0], k_rows, loc.at[0]),
        pltpu.make_async_copy(v_hbm.at[0], v_rows, loc.at[1]),
        pltpu.make_async_copy(q_hbm.at[0], q_rows, loc.at[2]),
        pltpu.make_async_copy(small_hbm.at[0], routes, loc.at[5]),
    ]
    for load in loads:
        load.start()

    def at(row, column):
        return {"seq": row % NY * NZ + column % NZ}

    right, left = at(y, z + 1), at(y, z + NZ - 1)

    def peer(dy):
        return at(y + dy, z)

    def remote(src, dst, send, recv, device):
        return pltpu.make_async_remote_copy(
            src_ref=src, dst_ref=dst, send_sem=send, recv_sem=recv,
            device_id=device, device_id_type=MESH,
        )

    barrier = pltpu.get_barrier_semaphore()
    for device in [right, left] + [peer(dy) for dy in range(1, NY)]:
        pl.semaphore_signal(barrier, inc=1, device_id=device, device_id_type=MESH)

    def chunk_right(s, c):
        return remote(kv.at[s - 1, c], kv.at[s, c], rs.at[s, c], rr.at[s, c], right)

    def chunk_left(s, c):
        pair = (c + SPLIT) % HP
        return remote(
            kv.at[(NZ + 1 - s) % NZ, pair], kv.at[NZ - s, pair], ls.at[s, c], lr.at[s, c], left
        )

    def tis_right(s):
        return remote(tis.at[s - 1], tis.at[s], trs.at[s], trr.at[s], right)

    def tis_left(s):
        return remote(tis.at[(NZ + 1 - s) % NZ], tis.at[NZ - s], tls.at[s], tlr.at[s], left)

    def tab_copy(dy):
        back = (NY - dy) % NY
        return remote(tab.at[dy], tabv.at[back], t_send.at[dy], t_recv.at[back], peer(dy))

    half = UNITS // 2

    def q_up(part):
        units = pl.ds(part * half, half)
        return remote(qs.at[0, units], qs.at[NY - 1, units], q_send.at[0, part], q_recv.at[0, part], peer(1))

    def q_down(part):
        units = pl.ds(part * half, half)
        return remote(qs.at[0, units], qs.at[1, units], q_send.at[1, part], q_recv.at[1, part], peer(NY - 1))

    def q_on_up():
        units = pl.ds(0, half)
        return remote(qs.at[NY - 1, units], qs.at[2, units], q_send.at[2, 0], q_recv.at[2, 0], peer(1))

    def q_on_down():
        units = pl.ds(half, half)
        return remote(qs.at[1, units], qs.at[2, units], q_send.at[2, 1], q_recv.at[2, 1], peer(NY - 1))

    def lay_pair(g):
        columns = slice(g * PAIR, (g + 1) * PAIR)
        for t in range(2):
            tokens = slice(t * TILE, (t + 1) * TILE)
            kv[0, g, t] = k_rows[tokens, columns]
            kv[0, g, 2 + t] = v_rows[tokens, columns].T

    loads[0].wait()
    loads[1].wait()
    for c in range(HP):
        if c < SPLIT:
            lay_pair(c)
            lay_pair(c + SPLIT)
        if c == 0:
            pl.semaphore_wait(barrier, 2 + NY - 1)
        if c < AHEAD:
            chunk_right(1, c).start()
            chunk_left(1, c).start()

    for load in loads[3:]:
        load.wait()
    for t in range(2):
        tis[0, t] = jnp.full((8, 128), (routes[SPAN, t] == 1).astype(jnp.int32), jnp.int32)
    tis_right(1).start()
    tis_left(1).start()

    lane = lax.broadcasted_iota(jnp.int32, (8, 128), 1)
    row = lax.broadcasted_iota(jnp.int32, (8, 128), 0)
    block = (y + row) % NY * NZ + (z + NZ - (lane // 2) % NZ) % NZ
    first = jnp.full((8, 128), UNITS - 1, jnp.int32)
    last = jnp.zeros((8, 128), jnp.int32)
    for u in range(UNITS):
        named = block == routes[0, u]
        for j in range(1, SPAN):
            named = named | (block == routes[j, u])
        first = jnp.where(named, jnp.minimum(first, u), first)
        last = jnp.where(named, u, last)
    table = jnp.where(lane % 2 == 0, first, last)
    for dy in range(NY):
        tab[dy] = jnp.broadcast_to(table[dy : dy + 1], (8, 128))
    for dy in range(1, NY):
        tab_copy(dy).start()

    scale = jnp.bfloat16((PAIR // 2) ** -0.5)
    loads[2].wait()

    def lay_queries(part):
        for i in range(half):
            u = part * half + i
            tile, g = u // HP, u % HP
            qs[0, u] = (q_rows[tile * TILE : (tile + 1) * TILE, g * PAIR : (g + 1) * PAIR] * scale).T

    lay_queries(0)
    q_up(0).start()
    lay_queries(1)
    q_down(1).start()
    q_up(1).start()
    q_down(0).start()

    def own_units(low, count):
        numbers = [low + i for i in range(count)]

        def scores_of(u):
            return jnp.dot(
                kv[0, u % HP, u // HP], halves(qs[0, u]), preferred_element_type=jnp.float32
            )

        scores = scores_of(numbers[0])
        done = []
        for i, u in enumerate(numbers):
            later = scores_of(numbers[i + 1]) if i + 1 < count else None
            shift = jnp.max(scores, axis=0, keepdims=True)
            probs = jnp.exp(scores - shift)
            total = jnp.sum(probs, axis=0, keepdims=True)
            both = jnp.dot(
                kv[0, u % HP, 2 + u // HP], probs.astype(jnp.bfloat16), preferred_element_type=jnp.float32
            )
            done.append((u, fold(both), by_head(shift) + by_head(total)))
            scores = later
        for u, folded, four in done:
            own_acc[u] = folded
            own_stat[u] = jnp.concatenate(four + four, axis=0)

    def slots(jobs):
        def scores_of(job):
            work, d, dy, c = job
            u = tabs[dy, 0, d * 2 + c]
            g = u & (HP - 1)
            unit = halves(qs[dy, u])
            keep = []
            for t in range(2):
                row = tis[d, t, 0:1, :]
                if work is work_o:
                    row = row * (1 - ((dy == 0) & ((u >> 3) == t)).astype(jnp.int32))
                keep.append(jnp.concatenate([row, row], axis=1) != 0)
            value = jnp.concatenate([work[g, 2], work[g, 3]], axis=1)
            keys = jnp.concatenate([work[g, 0], work[g, 1]], axis=0)
            both = jnp.dot(keys, unit, preferred_element_type=jnp.float32)
            return [both[:TILE], both[TILE:]], keep, value

        ready = scores_of(jobs[0])
        done = []
        for i, job in enumerate(jobs):
            later = scores_of(jobs[i + 1]) if i + 1 < len(jobs) else None
            scores, keep, value = ready
            peaks = [
                jnp.where(keep[t], jnp.max(scores[t], axis=0, keepdims=True), big_negative)
                for t in range(2)
            ]
            shift = jnp.maximum(peaks[0], peaks[1]).astype(jnp.bfloat16).astype(jnp.float32)
            weights = [
                jnp.exp(scores[t] - jnp.where(keep[t], shift, -big_negative)) for t in range(2)
            ]
            total = jnp.sum(weights[0], axis=0, keepdims=True) + jnp.sum(weights[1], axis=0, keepdims=True)
            both = jnp.dot(
                value,
                jnp.concatenate([w.astype(jnp.bfloat16) for w in weights], axis=0),
                preferred_element_type=jnp.float32,
            )
            four = by_head(shift) + by_head(total)
            done.append((job, fold(both), jnp.concatenate(four * 2, axis=0)))
            ready = later
        for i, ((work, d, dy, c), folded, stat) in enumerate(done):
            pieces = folded.astype(jnp.bfloat16).reshape(PIECES, PIECE, TILE)
            ret_out[dy, d, c * PIECES : (c + 1) * PIECES] = pieces
            if c == 1:
                both = jnp.concatenate([done[i - 1][2], stat], axis=0)
                ret_out[dy, d, 2 * PIECES] = both.astype(jnp.bfloat16)

    def ret_copy(dy, d):
        back = (NY - dy) % NY
        return remote(
            ret_out.at[dy, d], ret_in.at[back * NZ + d], ret_s.at[dy, d], ret_r.at[back, d], peer(dy)
        )

    def ret_local(d):
        return pltpu.make_async_copy(ret_out.at[0, d], ret_in.at[d], ret_r.at[0, d])

    def give_back(dy, d):
        @pl.when(dy == 0)
        def _():
            ret_local(d).start()

        @pl.when(dy > 0)
        def _():
            ret_copy(dy, d).start()

    def ret_wait(d):
        ret_local(d).wait()
        for dy in range(1, NY):
            ret_copy(dy, d).wait_send()
            ret_copy(dy, d).wait_recv()

    def fill(work, d):
        for g in range(HP):
            work[g] = kv[d, g]

    def relay(s, c):
        later, chunk = s + (c + AHEAD) // HP, (c + AHEAD) % HP
        chunk_right(s, c).wait_send()
        chunk_left(s, c).wait_send()

        @pl.when((later < HALF) | (chunk < SPLIT))
        def _():
            chunk_right(later, chunk).start()
            chunk_left(later, chunk).start()

        chunk_right(s, c).wait_recv()
        chunk_left(s, c).wait_recv()

    def relay_tissue(s):
        tis_right(s).wait_recv()
        tis_right(s + 1).start()
        tis_left(s).wait_recv()

        @pl.when(s < HALF - 1)
        def _():
            tis_left(s + 1).start()

        tis_right(s).wait_send()
        tis_left(s).wait_send()

    relay_tissue(1)

    def first_points(low, high):
        @pl.loop(low, high)
        def _(c):
            relay(1, c)
            own_units(2 * c, 2)

    first_points(0, HP - 3)
    q_up(0).wait_recv()
    q_on_up().start()
    q_down(1).wait_recv()
    q_on_down().start()
    first_points(HP - 3, HP)

    for dy in range(1, NY):
        tab_copy(dy).wait_recv()
    tabv[0] = tab[0]
    moves = [pltpu.make_async_copy(tabv, tabs, loc.at[3]), pltpu.make_async_copy(tab, tabo, loc.at[4])]
    for move in moves:
        move.start()
    for move in moves:
        move.wait()
    q_up(1).wait_recv()
    q_down(0).wait_recv()
    q_on_up().wait_recv()
    q_on_down().wait_recv()
    fill(work_o, 0)

    def find_places():
        @pl.loop(0, UNITS)
        def _(u):
            for j in range(SPAN):
                b = routes[j, u]
                dy = ((b >> 4) + NY - y) & (NY - 1)
                d = (z + NZ - (b & (NZ - 1))) & (NZ - 1)
                places[2 * (u * SPAN + j)] = dy * NZ + d
                places[2 * (u * SPAN + j) + 1] = (tabo[dy, 0, 2 * d] != u).astype(jnp.int32)

    @pl.loop(2, HALF + 1)
    def _(s):
        before_r, before_l = s - 1, NZ + 1 - s

        @pl.when(s < HALF)
        def _():
            relay_tissue(s)

        fill(work_r, before_r)
        fill(work_l, before_l)

        @pl.when(s == 3)
        def _():
            find_places()
            for dy in range(1, NY):
                tab_copy(dy).wait_send()
            for part in range(2):
                q_up(part).wait_send()
                q_down(part).wait_send()
            q_on_up().wait_send()
            q_on_down().wait_send()

        @pl.when(s == 4)
        def _():
            ret_wait(0)

        @pl.when(s >= 4)
        def _():
            ret_wait(s - 3)
            ret_wait(NZ + 3 - s)

        @pl.loop(0, NY)
        def _(dy):
            @pl.when(s < HALF)
            def _():
                relay(s, 2 * dy)

            slots([(work_r, before_r, dy, c) for c in range(2)])
            give_back(dy, before_r)

            @pl.when(s < HALF)
            def _():
                relay(s, 2 * dy + 1)

            slots([(work_l, before_l, dy, c) for c in range(2)])
            give_back(dy, before_l)

            @pl.when(s == 2)
            def _():
                slots([(work_o, 0, dy, c) for c in range(2)])
                give_back(dy, 0)

    tis_right(HALF).wait_send()
    tis_right(HALF).wait_recv()
    for d in (HALF - 2, HALF + 2, HALF - 1, HALF + 1):
        ret_wait(d)

    for c in range(SPLIT):
        chunk_right(HALF, c).wait_recv()
        work_r[c] = kv[HALF, c]
        chunk_left(HALF, c).wait_recv()
        work_r[c + SPLIT] = kv[HALF, c + SPLIT]

    @pl.loop(0, NY // 2)
    def _(i):
        pair = [2 + i, 1 - i]
        slots([(work_r, HALF, dy, c) for dy in pair for c in range(2)])
        for dy in pair:
            give_back(dy, HALF)

    for c in range(SPLIT):
        chunk_right(HALF, c).wait_send()
        chunk_left(HALF, c).wait_send()
    ret_wait(HALF)

    mid = PAIR // 2

    def combine(u):
        tile, g = u // HP, u % HP
        spots = [(places[2 * (u * SPAN + j)], places[2 * (u * SPAN + j) + 1]) for j in range(SPAN)]
        stats = []
        for a, c in spots:
            both = ret_in[a, 2 * PIECES].astype(jnp.float32)
            stats.append(jnp.where(c == 0, both[0:8], both[8:16]))
        own = own_stat[u]
        rows = []
        for h in range(2):
            span = slice(h * mid, (h + 1) * mid)
            shifts = [st[h : h + 1, :] for st in stats]
            totals = [st[2 + h : 3 + h, :] for st in stats]
            top = own[h : h + 1, :]
            for sh in shifts:
                top = jnp.maximum(top, sh)
            own_w = jnp.exp(own[h : h + 1, :] - top)
            ws = [jnp.exp(sh - top) for sh in shifts]
            den = own_w * own[2 + h : 3 + h, :]
            for w, t in zip(ws, totals):
                den = den + w * t
            inv = 1.0 / den
            num = own_acc[u, span, :] * (own_w * inv)
            for (a, c), w in zip(spots, ws):
                first = c * PIECES + h * (PIECES // 2)
                part = jnp.concatenate([ret_in[a, first + i] for i in range(PIECES // 2)], axis=0)
                num = num + part.astype(jnp.float32) * (w * inv)
            rows.append(num)
        result = jnp.concatenate(rows, axis=0)
        rows_at = pl.ds(pl.multiple_of(tile * TILE, TILE), TILE)
        out[rows_at, pl.ds(pl.multiple_of(g * PAIR, PAIR), PAIR)] = result.T.astype(jnp.bfloat16)

    @pl.loop(0, UNITS // 4)
    def _(i):
        for k in range(4):
            combine(4 * i + k)


def local(queries, key_rows, values, tissue, routes):
    wide = jnp.pad(tissue[:, None], ((0, 0), (0, 0), (0, UNITS - tissue.shape[1])))
    small = jnp.concatenate([routes.transpose(0, 2, 1), wide], axis=1)
    vmem = pl.BlockSpec(memory_space=pltpu.VMEM)
    hbm = pl.BlockSpec(memory_space=pltpu.HBM)
    dma = pltpu.SemaphoreType.DMA
    steps = HALF + 1
    rows = (2 * TILE, HP * PAIR)
    block = (HP, 4, PAIR, TILE)
    out = pl.pallas_call(
        kernel,
        out_shape=jax.ShapeDtypeStruct(rows, jnp.bfloat16),
        in_specs=[hbm] * 4,
        out_specs=vmem,
        scratch_shapes=[
            pltpu.SMEM((SPAN + 1, UNITS), jnp.int32),
            pltpu.VMEM(rows, jnp.bfloat16),
            pltpu.VMEM(rows, jnp.bfloat16),
            pltpu.VMEM(rows, jnp.bfloat16),
            pltpu.VMEM((NZ,) + block, jnp.bfloat16),
            pltpu.VMEM((NZ, 2, 8, 128), jnp.int32),
            pltpu.VMEM(block, jnp.bfloat16),
            pltpu.VMEM(block, jnp.bfloat16),
            pltpu.VMEM(block, jnp.bfloat16),
            pltpu.VMEM((NY, UNITS, PAIR, TILE), jnp.bfloat16),
            pltpu.VMEM((NY, 8, 128), jnp.int32),
            pltpu.VMEM((NY, 8, 128), jnp.int32),
            pltpu.SMEM((NY, 8, 128), jnp.int32),
            pltpu.SMEM((NY, 8, 128), jnp.int32),
            pltpu.SMEM((2 * UNITS * SPAN,), jnp.int32),
            pltpu.VMEM((NY, NZ, 2 * PIECES + 1, PIECE, TILE), jnp.bfloat16),
            pltpu.VMEM((NY * NZ, 2 * PIECES + 1, PIECE, TILE), jnp.bfloat16),
            pltpu.VMEM((UNITS, PAIR, TILE), jnp.float32),
            pltpu.VMEM((UNITS, 8, 128), jnp.float32),
            dma((steps, HP)), dma((steps, HP)), dma((steps, HP)), dma((steps, HP)),
            dma((steps,)), dma((steps,)), dma((steps,)), dma((steps,)),
            dma((3, 2)), dma((3, 2)), dma((NY,)), dma((NY,)),
            dma((NY, NZ)), dma((NY, NZ)), dma((6,)),
        ],
        compiler_params=pltpu.CompilerParams(
            collective_id=0, has_side_effects=True, vmem_limit_bytes=53 * 1024 * 1024
        ),
    )(small, queries, key_rows, values)
    return out[None]


def solution(mesh):
    placed = (
        P("slide", "seq", None),
        P("slide", "seq", None),
        P("slide", "seq", None),
        P("slide", "seq"),
        P("slide", "seq", None),
    )
    return jax.shard_map(
        local, mesh=mesh, in_specs=placed, out_specs=P("slide", "seq", None), check_vma=False
    )
```

```python
import jax
import jax.numpy as jnp
from jax import lax
from jax.experimental import pallas as pl
from jax.experimental.pallas import tpu as pltpu
from jax.sharding import PartitionSpec as P

NY = 4
NZ = 16
TILE = 128
HP = 8
PAIR = 128
HALF = NZ // 2
SPLIT = HP // 2
AHEAD = 7
UNITS = 16
SPAN = 4
PIECE = 16
PIECES = PAIR // PIECE

big_negative = -1e30
MESH = pl.DeviceIdType.MESH


def halves(unit):
    mid = PAIR // 2
    zero = jnp.zeros((mid, TILE), unit.dtype)
    upper = jnp.concatenate([unit[:mid], zero], axis=1)
    return jnp.concatenate([upper, jnp.concatenate([zero, unit[mid:]], axis=1)], axis=0)


def fold(both):
    mid = PAIR // 2
    return jnp.concatenate([both[:mid, :TILE], both[mid:, TILE:]], axis=0)


def by_head(pair_row):
    return pair_row[:, :TILE], pair_row[:, TILE:]


def kernel(
    small_hbm, q_hbm, k_hbm, v_hbm, out,
    routes, q_rows, k_rows, v_rows, kv, tis, work_o, work_r, work_l, qs, tab, tabv, tabs, tabo, places,
    ret_out, ret_in, own_acc, own_stat,
    rs, rr, ls, lr, trs, trr, tls, tlr, q_send, q_recv, t_send, t_recv, ret_s, ret_r, loc,
):
    me = lax.axis_index("seq")
    y, z = me // NZ, me % NZ

    loads = [
        pltpu.make_async_copy(k_hbm.at[0], k_rows, loc.at[0]),
        pltpu.make_async_copy(v_hbm.at[0], v_rows, loc.at[1]),
        pltpu.make_async_copy(q_hbm.at[0], q_rows, loc.at[2]),
        pltpu.make_async_copy(small_hbm.at[0], routes, loc.at[5]),
    ]
    for load in loads:
        load.start()

    def at(row, column):
        return {"seq": row % NY * NZ + column % NZ}

    right, left = at(y, z + 1), at(y, z + NZ - 1)

    def peer(dy):
        return at(y + dy, z)

    def remote(src, dst, send, recv, device):
        return pltpu.make_async_remote_copy(
            src_ref=src, dst_ref=dst, send_sem=send, recv_sem=recv,
            device_id=device, device_id_type=MESH,
        )

    barrier = pltpu.get_barrier_semaphore()
    for device in [right, left] + [peer(dy) for dy in range(1, NY)]:
        pl.semaphore_signal(barrier, inc=1, device_id=device, device_id_type=MESH)

    def chunk_right(s, c):
        return remote(kv.at[s - 1, c], kv.at[s, c], rs.at[s, c], rr.at[s, c], right)

    def chunk_left(s, c):
        pair = (c + SPLIT) % HP
        return remote(
            kv.at[(NZ + 1 - s) % NZ, pair], kv.at[NZ - s, pair], ls.at[s, c], lr.at[s, c], left
        )

    def tis_right(s):
        return remote(tis.at[s - 1], tis.at[s], trs.at[s], trr.at[s], right)

    def tis_left(s):
        return remote(tis.at[(NZ + 1 - s) % NZ], tis.at[NZ - s], tls.at[s], tlr.at[s], left)

    def tab_copy(dy):
        back = (NY - dy) % NY
        return remote(tab.at[dy], tabv.at[back], t_send.at[dy], t_recv.at[back], peer(dy))

    half = UNITS // 2

    def q_up(part):
        units = pl.ds(part * half, half)
        return remote(qs.at[0, units], qs.at[NY - 1, units], q_send.at[0, part], q_recv.at[0, part], peer(1))

    def q_down(part):
        units = pl.ds(part * half, half)
        return remote(qs.at[0, units], qs.at[1, units], q_send.at[1, part], q_recv.at[1, part], peer(NY - 1))

    def q_on_up():
        units = pl.ds(0, half)
        return remote(qs.at[NY - 1, units], qs.at[2, units], q_send.at[2, 0], q_recv.at[2, 0], peer(1))

    def q_on_down():
        units = pl.ds(half, half)
        return remote(qs.at[1, units], qs.at[2, units], q_send.at[2, 1], q_recv.at[2, 1], peer(NY - 1))

    def lay_pair(g):
        columns = slice(g * PAIR, (g + 1) * PAIR)
        for t in range(2):
            tokens = slice(t * TILE, (t + 1) * TILE)
            kv[0, g, t] = k_rows[tokens, columns]
            kv[0, g, 2 + t] = v_rows[tokens, columns].T

    loads[0].wait()
    loads[1].wait()
    for c in range(HP):
        if c < SPLIT:
            lay_pair(c)
            lay_pair(c + SPLIT)
        if c == 0:
            pl.semaphore_wait(barrier, 2 + NY - 1)
        if c < AHEAD:
            chunk_right(1, c).start()
            chunk_left(1, c).start()

    for load in loads[3:]:
        load.wait()
    for t in range(2):
        tis[0, t] = jnp.full((8, 128), (routes[SPAN, t] == 1).astype(jnp.int32), jnp.int32)
    tis_right(1).start()
    tis_left(1).start()

    lane = lax.broadcasted_iota(jnp.int32, (8, 128), 1)
    row = lax.broadcasted_iota(jnp.int32, (8, 128), 0)
    block = (y + row) % NY * NZ + (z + NZ - (lane // 2) % NZ) % NZ
    first = jnp.full((8, 128), UNITS - 1, jnp.int32)
    last = jnp.zeros((8, 128), jnp.int32)
    for u in range(UNITS):
        named = block == routes[0, u]
        for j in range(1, SPAN):
            named = named | (block == routes[j, u])
        first = jnp.where(named, jnp.minimum(first, u), first)
        last = jnp.where(named, u, last)
    table = jnp.where(lane % 2 == 0, first, last)
    for dy in range(NY):
        tab[dy] = jnp.broadcast_to(table[dy : dy + 1], (8, 128))
    for dy in range(1, NY):
        tab_copy(dy).start()

    scale = jnp.bfloat16((PAIR // 2) ** -0.5)
    loads[2].wait()

    def lay_queries(part):
        for i in range(half):
            u = part * half + i
            tile, g = u // HP, u % HP
            qs[0, u] = (q_rows[tile * TILE : (tile + 1) * TILE, g * PAIR : (g + 1) * PAIR] * scale).T

    lay_queries(0)
    q_up(0).start()
    lay_queries(1)
    q_down(1).start()
    q_up(1).start()
    q_down(0).start()

    def own_units(low, count):
        numbers = [low + i for i in range(count)]

        def scores_of(u):
            return jnp.dot(
                kv[0, u % HP, u // HP], halves(qs[0, u]), preferred_element_type=jnp.float32
            )

        scores = scores_of(numbers[0])
        done = []
        for i, u in enumerate(numbers):
            later = scores_of(numbers[i + 1]) if i + 1 < count else None
            shift = jnp.max(scores, axis=0, keepdims=True)
            probs = jnp.exp(scores - shift)
            total = jnp.sum(probs, axis=0, keepdims=True)
            both = jnp.dot(
                kv[0, u % HP, 2 + u // HP], probs.astype(jnp.bfloat16), preferred_element_type=jnp.float32
            )
            done.append((u, fold(both), by_head(shift) + by_head(total)))
            scores = later
        for u, folded, four in done:
            own_acc[u] = folded
            own_stat[u] = jnp.concatenate(four + four, axis=0)

    def slots(jobs):
        def scores_of(job):
            work, d, dy, c = job
            u = tabs[dy, 0, d * 2 + c]
            g = u & (HP - 1)
            unit = halves(qs[dy, u])
            keep = []
            for t in range(2):
                row = tis[d, t, 0:1, :]
                if work is work_o:
                    row = row * (1 - ((dy == 0) & ((u >> 3) == t)).astype(jnp.int32))
                keep.append(jnp.concatenate([row, row], axis=1) != 0)
            value = jnp.concatenate([work[g, 2], work[g, 3]], axis=1)
            keys = jnp.concatenate([work[g, 0], work[g, 1]], axis=0)
            both = jnp.dot(keys, unit, preferred_element_type=jnp.float32)
            return [both[:TILE], both[TILE:]], keep, value

        ready = scores_of(jobs[0])
        done = []
        for i, job in enumerate(jobs):
            later = scores_of(jobs[i + 1]) if i + 1 < len(jobs) else None
            scores, keep, value = ready
            peaks = [
                jnp.where(keep[t], jnp.max(scores[t], axis=0, keepdims=True), big_negative)
                for t in range(2)
            ]
            shift = jnp.maximum(peaks[0], peaks[1]).astype(jnp.bfloat16).astype(jnp.float32)
            weights = [
                jnp.exp(scores[t] - jnp.where(keep[t], shift, -big_negative)) for t in range(2)
            ]
            total = jnp.sum(weights[0], axis=0, keepdims=True) + jnp.sum(weights[1], axis=0, keepdims=True)
            both = jnp.dot(
                value,
                jnp.concatenate([w.astype(jnp.bfloat16) for w in weights], axis=0),
                preferred_element_type=jnp.float32,
            )
            four = by_head(shift) + by_head(total)
            done.append((job, fold(both), jnp.concatenate(four * 2, axis=0)))
            ready = later
        for i, ((work, d, dy, c), folded, stat) in enumerate(done):
            pieces = folded.astype(jnp.bfloat16).reshape(PIECES, PIECE, TILE)
            ret_out[dy, d, c * PIECES : (c + 1) * PIECES] = pieces
            if c == 1:
                both = jnp.concatenate([done[i - 1][2], stat], axis=0)
                ret_out[dy, d, 2 * PIECES] = both.astype(jnp.bfloat16)

    def ret_copy(dy, d):
        back = (NY - dy) % NY
        return remote(
            ret_out.at[dy, d], ret_in.at[back * NZ + d], ret_s.at[dy, d], ret_r.at[back, d], peer(dy)
        )

    def ret_local(d):
        return pltpu.make_async_copy(ret_out.at[0, d], ret_in.at[d], ret_r.at[0, d])

    def give_back(dy, d):
        @pl.when(dy == 0)
        def _():
            ret_local(d).start()

        @pl.when(dy > 0)
        def _():
            ret_copy(dy, d).start()

    def ret_wait(d):
        ret_local(d).wait()
        for dy in range(1, NY):
            ret_copy(dy, d).wait_send()
            ret_copy(dy, d).wait_recv()

    def fill(work, d):
        for g in range(HP):
            work[g] = kv[d, g]

    def relay(s, c):
        later, chunk = s + (c + AHEAD) // HP, (c + AHEAD) % HP
        chunk_right(s, c).wait_send()
        chunk_left(s, c).wait_send()

        @pl.when((later < HALF) | (chunk < SPLIT))
        def _():
            chunk_right(later, chunk).start()
            chunk_left(later, chunk).start()

        chunk_right(s, c).wait_recv()
        chunk_left(s, c).wait_recv()

    def relay_tissue(s):
        tis_right(s).wait_recv()
        tis_right(s + 1).start()
        tis_left(s).wait_recv()

        @pl.when(s < HALF - 1)
        def _():
            tis_left(s + 1).start()

        tis_right(s).wait_send()
        tis_left(s).wait_send()

    relay_tissue(1)

    def first_points(low, high):
        @pl.loop(low, high)
        def _(c):
            relay(1, c)
            own_units(2 * c, 2)

    first_points(0, HP - 3)
    q_up(0).wait_recv()
    q_on_up().start()
    q_down(1).wait_recv()
    q_on_down().start()
    first_points(HP - 3, HP)

    for dy in range(1, NY):
        tab_copy(dy).wait_recv()
    tabv[0] = tab[0]
    moves = [pltpu.make_async_copy(tabv, tabs, loc.at[3]), pltpu.make_async_copy(tab, tabo, loc.at[4])]
    for move in moves:
        move.start()
    for move in moves:
        move.wait()
    q_up(1).wait_recv()
    q_down(0).wait_recv()
    q_on_up().wait_recv()
    q_on_down().wait_recv()
    fill(work_o, 0)

    def find_places():
        @pl.loop(0, UNITS)
        def _(u):
            for j in range(SPAN):
                b = routes[j, u]
                dy = ((b >> 4) + NY - y) & (NY - 1)
                d = (z + NZ - (b & (NZ - 1))) & (NZ - 1)
                places[2 * (u * SPAN + j)] = dy * NZ + d
                places[2 * (u * SPAN + j) + 1] = (tabo[dy, 0, 2 * d] != u).astype(jnp.int32)

    @pl.loop(2, HALF + 1)
    def _(s):
        before_r, before_l = s - 1, NZ + 1 - s

        @pl.when(s < HALF)
        def _():
            relay_tissue(s)

        fill(work_r, before_r)
        fill(work_l, before_l)

        @pl.when(s == 3)
        def _():
            find_places()
            for dy in range(1, NY):
                tab_copy(dy).wait_send()
            for part in range(2):
                q_up(part).wait_send()
                q_down(part).wait_send()
            q_on_up().wait_send()
            q_on_down().wait_send()

        @pl.when(s == 4)
        def _():
            ret_wait(0)

        @pl.when(s >= 4)
        def _():
            ret_wait(s - 3)
            ret_wait(NZ + 3 - s)

        @pl.loop(0, NY)
        def _(dy):
            @pl.when(s < HALF)
            def _():
                relay(s, 2 * dy)

            slots([(work_r, before_r, dy, c) for c in range(2)])
            give_back(dy, before_r)

            @pl.when(s < HALF)
            def _():
                relay(s, 2 * dy + 1)

            slots([(work_l, before_l, dy, c) for c in range(2)])
            give_back(dy, before_l)

            @pl.when(s == 3)
            def _():
                slots([(work_o, 0, dy, c) for c in range(2)])
                give_back(dy, 0)

    tis_right(HALF).wait_send()
    tis_right(HALF).wait_recv()
    for d in (HALF - 2, HALF + 2, HALF - 1, HALF + 1):
        ret_wait(d)

    for c in range(SPLIT):
        chunk_right(HALF, c).wait_recv()
        work_r[c] = kv[HALF, c]
        chunk_left(HALF, c).wait_recv()
        work_r[c + SPLIT] = kv[HALF, c + SPLIT]

    @pl.loop(0, NY // 2)
    def _(i):
        pair = [2 + i, 1 - i]
        slots([(work_r, HALF, dy, c) for dy in pair for c in range(2)])
        for dy in pair:
            give_back(dy, HALF)

    for c in range(SPLIT):
        chunk_right(HALF, c).wait_send()
        chunk_left(HALF, c).wait_send()
    ret_wait(HALF)

    mid = PAIR // 2

    def combine(u):
        tile, g = u // HP, u % HP
        spots = [(places[2 * (u * SPAN + j)], places[2 * (u * SPAN + j) + 1]) for j in range(SPAN)]
        stats = []
        for a, c in spots:
            both = ret_in[a, 2 * PIECES].astype(jnp.float32)
            stats.append(jnp.where(c == 0, both[0:8], both[8:16]))
        own = own_stat[u]
        rows = []
        for h in range(2):
            span = slice(h * mid, (h + 1) * mid)
            shifts = [st[h : h + 1, :] for st in stats]
            totals = [st[2 + h : 3 + h, :] for st in stats]
            top = own[h : h + 1, :]
            for sh in shifts:
                top = jnp.maximum(top, sh)
            own_w = jnp.exp(own[h : h + 1, :] - top)
            ws = [jnp.exp(sh - top) for sh in shifts]
            den = own_w * own[2 + h : 3 + h, :]
            for w, t in zip(ws, totals):
                den = den + w * t
            inv = 1.0 / den
            num = own_acc[u, span, :] * (own_w * inv)
            for (a, c), w in zip(spots, ws):
                first = c * PIECES + h * (PIECES // 2)
                part = jnp.concatenate([ret_in[a, first + i] for i in range(PIECES // 2)], axis=0)
                num = num + part.astype(jnp.float32) * (w * inv)
            rows.append(num)
        result = jnp.concatenate(rows, axis=0)
        rows_at = pl.ds(pl.multiple_of(tile * TILE, TILE), TILE)
        out[rows_at, pl.ds(pl.multiple_of(g * PAIR, PAIR), PAIR)] = result.T.astype(jnp.bfloat16)

    @pl.loop(0, UNITS // 4)
    def _(i):
        for k in range(4):
            combine(4 * i + k)


def local(queries, key_rows, values, tissue, routes):
    wide = jnp.pad(tissue[:, None], ((0, 0), (0, 0), (0, UNITS - tissue.shape[1])))
    small = jnp.concatenate([routes.transpose(0, 2, 1), wide], axis=1)
    vmem = pl.BlockSpec(memory_space=pltpu.VMEM)
    hbm = pl.BlockSpec(memory_space=pltpu.HBM)
    dma = pltpu.SemaphoreType.DMA
    steps = HALF + 1
    rows = (2 * TILE, HP * PAIR)
    block = (HP, 4, PAIR, TILE)
    out = pl.pallas_call(
        kernel,
        out_shape=jax.ShapeDtypeStruct(rows, jnp.bfloat16),
        in_specs=[hbm] * 4,
        out_specs=vmem,
        scratch_shapes=[
            pltpu.SMEM((SPAN + 1, UNITS), jnp.int32),
            pltpu.VMEM(rows, jnp.bfloat16),
            pltpu.VMEM(rows, jnp.bfloat16),
            pltpu.VMEM(rows, jnp.bfloat16),
            pltpu.VMEM((NZ,) + block, jnp.bfloat16),
            pltpu.VMEM((NZ, 2, 8, 128), jnp.int32),
            pltpu.VMEM(block, jnp.bfloat16),
            pltpu.VMEM(block, jnp.bfloat16),
            pltpu.VMEM(block, jnp.bfloat16),
            pltpu.VMEM((NY, UNITS, PAIR, TILE), jnp.bfloat16),
            pltpu.VMEM((NY, 8, 128), jnp.int32),
            pltpu.VMEM((NY, 8, 128), jnp.int32),
            pltpu.SMEM((NY, 8, 128), jnp.int32),
            pltpu.SMEM((NY, 8, 128), jnp.int32),
            pltpu.SMEM((2 * UNITS * SPAN,), jnp.int32),
            pltpu.VMEM((NY, NZ, 2 * PIECES + 1, PIECE, TILE), jnp.bfloat16),
            pltpu.VMEM((NY * NZ, 2 * PIECES + 1, PIECE, TILE), jnp.bfloat16),
            pltpu.VMEM((UNITS, PAIR, TILE), jnp.float32),
            pltpu.VMEM((UNITS, 8, 128), jnp.float32),
            dma((steps, HP)), dma((steps, HP)), dma((steps, HP)), dma((steps, HP)),
            dma((steps,)), dma((steps,)), dma((steps,)), dma((steps,)),
            dma((3, 2)), dma((3, 2)), dma((NY,)), dma((NY,)),
            dma((NY, NZ)), dma((NY, NZ)), dma((6,)),
        ],
        compiler_params=pltpu.CompilerParams(
            collective_id=0, has_side_effects=True, vmem_limit_bytes=53 * 1024 * 1024
        ),
    )(small, queries, key_rows, values)
    return out[None]


def solution(mesh):
    placed = (
        P("slide", "seq", None),
        P("slide", "seq", None),
        P("slide", "seq", None),
        P("slide", "seq"),
        P("slide", "seq", None),
    )
    return jax.shard_map(
        local, mesh=mesh, in_specs=placed, out_specs=P("slide", "seq", None), check_vma=False
    )
```

```python
import jax
import jax.numpy as jnp
from jax import lax
from jax.experimental import pallas as pl
from jax.experimental.pallas import tpu as pltpu
from jax.sharding import PartitionSpec as P

NY = 4
NZ = 16
TILE = 128
HP = 8
PAIR = 128
HALF = NZ // 2
SPLIT = HP // 2
AHEAD = 6
UNITS = 16
SPAN = 4
PIECE = 16
PIECES = PAIR // PIECE

big_negative = -1e30
MESH = pl.DeviceIdType.MESH


def halves(unit):
    mid = PAIR // 2
    zero = jnp.zeros((mid, TILE), unit.dtype)
    upper = jnp.concatenate([unit[:mid], zero], axis=1)
    return jnp.concatenate([upper, jnp.concatenate([zero, unit[mid:]], axis=1)], axis=0)


def fold(both):
    mid = PAIR // 2
    return jnp.concatenate([both[:mid, :TILE], both[mid:, TILE:]], axis=0)


def by_head(pair_row):
    return pair_row[:, :TILE], pair_row[:, TILE:]


def kernel(
    small_hbm, q_hbm, k_hbm, v_hbm, out,
    routes, q_rows, k_rows, v_rows, kv, tis, work_o, work_r, work_l, qs, tab, tabv, tabs, tabo, places,
    ret_out, ret_in, own_acc, own_stat,
    rs, rr, ls, lr, trs, trr, tls, tlr, q_send, q_recv, t_send, t_recv, ret_s, ret_r, loc,
):
    me = lax.axis_index("seq")
    y, z = me // NZ, me % NZ

    loads = [
        pltpu.make_async_copy(k_hbm.at[0], k_rows, loc.at[0]),
        pltpu.make_async_copy(v_hbm.at[0], v_rows, loc.at[1]),
        pltpu.make_async_copy(q_hbm.at[0], q_rows, loc.at[2]),
        pltpu.make_async_copy(small_hbm.at[0], routes, loc.at[5]),
    ]
    for load in loads:
        load.start()

    def at(row, column):
        return {"seq": row % NY * NZ + column % NZ}

    right, left = at(y, z + 1), at(y, z + NZ - 1)

    def peer(dy):
        return at(y + dy, z)

    def remote(src, dst, send, recv, device):
        return pltpu.make_async_remote_copy(
            src_ref=src, dst_ref=dst, send_sem=send, recv_sem=recv,
            device_id=device, device_id_type=MESH,
        )

    barrier = pltpu.get_barrier_semaphore()
    for device in [right, left] + [peer(dy) for dy in range(1, NY)]:
        pl.semaphore_signal(barrier, inc=1, device_id=device, device_id_type=MESH)

    def chunk_right(s, c):
        return remote(kv.at[s - 1, c], kv.at[s, c], rs.at[s, c], rr.at[s, c], right)

    def chunk_left(s, c):
        pair = (c + SPLIT) % HP
        return remote(
            kv.at[(NZ + 1 - s) % NZ, pair], kv.at[NZ - s, pair], ls.at[s, c], lr.at[s, c], left
        )

    def tis_right(s):
        return remote(tis.at[s - 1], tis.at[s], trs.at[s], trr.at[s], right)

    def tis_left(s):
        return remote(tis.at[(NZ + 1 - s) % NZ], tis.at[NZ - s], tls.at[s], tlr.at[s], left)

    def tab_copy(dy):
        back = (NY - dy) % NY
        return remote(tab.at[dy], tabv.at[back], t_send.at[dy], t_recv.at[back], peer(dy))

    half = UNITS // 2

    def q_up(part):
        units = pl.ds(part * half, half)
        return remote(qs.at[0, units], qs.at[NY - 1, units], q_send.at[0, part], q_recv.at[0, part], peer(1))

    def q_down(part):
        units = pl.ds(part * half, half)
        return remote(qs.at[0, units], qs.at[1, units], q_send.at[1, part], q_recv.at[1, part], peer(NY - 1))

    def q_on_up():
        units = pl.ds(0, half)
        return remote(qs.at[NY - 1, units], qs.at[2, units], q_send.at[2, 0], q_recv.at[2, 0], peer(1))

    def q_on_down():
        units = pl.ds(half, half)
        return remote(qs.at[1, units], qs.at[2, units], q_send.at[2, 1], q_recv.at[2, 1], peer(NY - 1))

    def lay_pair(g):
        columns = slice(g * PAIR, (g + 1) * PAIR)
        for t in range(2):
            tokens = slice(t * TILE, (t + 1) * TILE)
            kv[0, g, t] = k_rows[tokens, columns]
            kv[0, g, 2 + t] = v_rows[tokens, columns].T

    loads[0].wait()
    loads[1].wait()
    for c in range(HP):
        if c < SPLIT:
            lay_pair(c)
            lay_pair(c + SPLIT)
        if c == 0:
            pl.semaphore_wait(barrier, 2 + NY - 1)
        if c < AHEAD:
            chunk_right(1, c).start()
            chunk_left(1, c).start()

    for load in loads[3:]:
        load.wait()
    for t in range(2):
        tis[0, t] = jnp.full((8, 128), (routes[SPAN, t] == 1).astype(jnp.int32), jnp.int32)
    tis_right(1).start()
    tis_left(1).start()

    lane = lax.broadcasted_iota(jnp.int32, (8, 128), 1)
    row = lax.broadcasted_iota(jnp.int32, (8, 128), 0)
    block = (y + row) % NY * NZ + (z + NZ - (lane // 2) % NZ) % NZ
    first = jnp.full((8, 128), UNITS - 1, jnp.int32)
    last = jnp.zeros((8, 128), jnp.int32)
    for u in range(UNITS):
        named = block == routes[0, u]
        for j in range(1, SPAN):
            named = named | (block == routes[j, u])
        first = jnp.where(named, jnp.minimum(first, u), first)
        last = jnp.where(named, u, last)
    table = jnp.where(lane % 2 == 0, first, last)
    for dy in range(NY):
        tab[dy] = jnp.broadcast_to(table[dy : dy + 1], (8, 128))
    for dy in range(1, NY):
        tab_copy(dy).start()

    scale = jnp.bfloat16((PAIR // 2) ** -0.5)
    loads[2].wait()

    def lay_queries(part):
        for i in range(half):
            u = part * half + i
            tile, g = u // HP, u % HP
            qs[0, u] = (q_rows[tile * TILE : (tile + 1) * TILE, g * PAIR : (g + 1) * PAIR] * scale).T

    lay_queries(0)
    q_up(0).start()
    lay_queries(1)
    q_down(1).start()
    q_up(1).start()
    q_down(0).start()

    def own_units(low, count):
        numbers = [low + i for i in range(count)]

        def scores_of(u):
            return jnp.dot(
                kv[0, u % HP, u // HP], halves(qs[0, u]), preferred_element_type=jnp.float32
            )

        scores = scores_of(numbers[0])
        done = []
        for i, u in enumerate(numbers):
            later = scores_of(numbers[i + 1]) if i + 1 < count else None
            shift = jnp.max(scores, axis=0, keepdims=True)
            probs = jnp.exp(scores - shift)
            total = jnp.sum(probs, axis=0, keepdims=True)
            both = jnp.dot(
                kv[0, u % HP, 2 + u // HP], probs.astype(jnp.bfloat16), preferred_element_type=jnp.float32
            )
            done.append((u, fold(both), by_head(shift) + by_head(total)))
            scores = later
        for u, folded, four in done:
            own_acc[u] = folded
            own_stat[u] = jnp.concatenate(four + four, axis=0)

    def slots(jobs):
        def scores_of(job):
            work, d, dy, c = job
            u = tabs[dy, 0, d * 2 + c]
            g = u & (HP - 1)
            unit = halves(qs[dy, u])
            keep = []
            for t in range(2):
                row = tis[d, t, 0:1, :]
                if work is work_o:
                    row = row * (1 - ((dy == 0) & ((u >> 3) == t)).astype(jnp.int32))
                keep.append(jnp.concatenate([row, row], axis=1) != 0)
            value = jnp.concatenate([work[g, 2], work[g, 3]], axis=1)
            keys = jnp.concatenate([work[g, 0], work[g, 1]], axis=0)
            both = jnp.dot(keys, unit, preferred_element_type=jnp.float32)
            return [both[:TILE], both[TILE:]], keep, value

        ready = scores_of(jobs[0])
        done = []
        for i, job in enumerate(jobs):
            later = scores_of(jobs[i + 1]) if i + 1 < len(jobs) else None
            scores, keep, value = ready
            peaks = [
                jnp.where(keep[t], jnp.max(scores[t], axis=0, keepdims=True), big_negative)
                for t in range(2)
            ]
            shift = jnp.maximum(peaks[0], peaks[1]).astype(jnp.bfloat16).astype(jnp.float32)
            weights = [
                jnp.exp(scores[t] - jnp.where(keep[t], shift, -big_negative)) for t in range(2)
            ]
            total = jnp.sum(weights[0], axis=0, keepdims=True) + jnp.sum(weights[1], axis=0, keepdims=True)
            both = jnp.dot(
                value,
                jnp.concatenate([w.astype(jnp.bfloat16) for w in weights], axis=0),
                preferred_element_type=jnp.float32,
            )
            four = by_head(shift) + by_head(total)
            done.append((job, fold(both), jnp.concatenate(four * 2, axis=0)))
            ready = later
        for i, ((work, d, dy, c), folded, stat) in enumerate(done):
            pieces = folded.astype(jnp.bfloat16).reshape(PIECES, PIECE, TILE)
            ret_out[dy, d, c * PIECES : (c + 1) * PIECES] = pieces
            if c == 1:
                both = jnp.concatenate([done[i - 1][2], stat], axis=0)
                ret_out[dy, d, 2 * PIECES] = both.astype(jnp.bfloat16)

    def ret_copy(dy, d):
        back = (NY - dy) % NY
        return remote(
            ret_out.at[dy, d], ret_in.at[back * NZ + d], ret_s.at[dy, d], ret_r.at[back, d], peer(dy)
        )

    def ret_local(d):
        return pltpu.make_async_copy(ret_out.at[0, d], ret_in.at[d], ret_r.at[0, d])

    def give_back(dy, d):
        @pl.when(dy == 0)
        def _():
            ret_local(d).start()

        @pl.when(dy > 0)
        def _():
            ret_copy(dy, d).start()

    def ret_wait(d):
        ret_local(d).wait()
        for dy in range(1, NY):
            ret_copy(dy, d).wait_send()
            ret_copy(dy, d).wait_recv()

    def fill(work, d):
        for g in range(HP):
            work[g] = kv[d, g]

    def relay(s, c):
        later, chunk = s + (c + AHEAD) // HP, (c + AHEAD) % HP
        chunk_right(s, c).wait_send()
        chunk_left(s, c).wait_send()

        @pl.when((later < HALF) | (chunk < SPLIT))
        def _():
            chunk_right(later, chunk).start()
            chunk_left(later, chunk).start()

        chunk_right(s, c).wait_recv()
        chunk_left(s, c).wait_recv()

    def relay_tissue(s):
        tis_right(s).wait_recv()
        tis_right(s + 1).start()
        tis_left(s).wait_recv()

        @pl.when(s < HALF - 1)
        def _():
            tis_left(s + 1).start()

        tis_right(s).wait_send()
        tis_left(s).wait_send()

    relay_tissue(1)

    def first_points(low, high):
        @pl.loop(low, high)
        def _(c):
            relay(1, c)
            own_units(2 * c, 2)

    first_points(0, HP - 3)
    q_up(0).wait_recv()
    q_on_up().start()
    q_down(1).wait_recv()
    q_on_down().start()
    first_points(HP - 3, HP)

    for dy in range(1, NY):
        tab_copy(dy).wait_recv()
    tabv[0] = tab[0]
    moves = [pltpu.make_async_copy(tabv, tabs, loc.at[3]), pltpu.make_async_copy(tab, tabo, loc.at[4])]
    for move in moves:
        move.start()
    for move in moves:
        move.wait()
    q_up(1).wait_recv()
    q_down(0).wait_recv()
    q_on_up().wait_recv()
    q_on_down().wait_recv()
    fill(work_o, 0)

    def find_places():
        @pl.loop(0, UNITS)
        def _(u):
            for j in range(SPAN):
                b = routes[j, u]
                dy = ((b >> 4) + NY - y) & (NY - 1)
                d = (z + NZ - (b & (NZ - 1))) & (NZ - 1)
                places[2 * (u * SPAN + j)] = dy * NZ + d
                places[2 * (u * SPAN + j) + 1] = (tabo[dy, 0, 2 * d] != u).astype(jnp.int32)

    @pl.loop(2, HALF + 1)
    def _(s):
        before_r, before_l = s - 1, NZ + 1 - s

        @pl.when(s < HALF)
        def _():
            relay_tissue(s)

        fill(work_r, before_r)
        fill(work_l, before_l)

        @pl.when(s == 3)
        def _():
            find_places()
            for dy in range(1, NY):
                tab_copy(dy).wait_send()
            for part in range(2):
                q_up(part).wait_send()
                q_down(part).wait_send()
            q_on_up().wait_send()
            q_on_down().wait_send()

        @pl.when(s == 4)
        def _():
            ret_wait(0)

        @pl.when(s >= 4)
        def _():
            ret_wait(s - 3)
            ret_wait(NZ + 3 - s)

        @pl.loop(0, NY)
        def _(dy):
            @pl.when(s < HALF)
            def _():
                relay(s, 2 * dy)

            slots([(work_r, before_r, dy, c) for c in range(2)])
            give_back(dy, before_r)

            @pl.when(s < HALF)
            def _():
                relay(s, 2 * dy + 1)

            slots([(work_l, before_l, dy, c) for c in range(2)])
            give_back(dy, before_l)

            @pl.when(s == 2)
            def _():
                slots([(work_o, 0, dy, c) for c in range(2)])
                give_back(dy, 0)

    tis_right(HALF).wait_send()
    tis_right(HALF).wait_recv()
    for d in (HALF - 2, HALF + 2, HALF - 1, HALF + 1):
        ret_wait(d)

    for c in range(SPLIT):
        chunk_right(HALF, c).wait_recv()
        work_r[c] = kv[HALF, c]
        chunk_left(HALF, c).wait_recv()
        work_r[c + SPLIT] = kv[HALF, c + SPLIT]

    @pl.loop(0, NY // 2)
    def _(i):
        pair = [2 + i, 1 - i]
        slots([(work_r, HALF, dy, c) for dy in pair for c in range(2)])
        for dy in pair:
            give_back(dy, HALF)

    for c in range(SPLIT):
        chunk_right(HALF, c).wait_send()
        chunk_left(HALF, c).wait_send()
    ret_wait(HALF)

    mid = PAIR // 2

    def combine(u):
        tile, g = u // HP, u % HP
        spots = [(places[2 * (u * SPAN + j)], places[2 * (u * SPAN + j) + 1]) for j in range(SPAN)]
        stats = []
        for a, c in spots:
            both = ret_in[a, 2 * PIECES].astype(jnp.float32)
            stats.append(jnp.where(c == 0, both[0:8], both[8:16]))
        own = own_stat[u]
        rows = []
        for h in range(2):
            span = slice(h * mid, (h + 1) * mid)
            shifts = [st[h : h + 1, :] for st in stats]
            totals = [st[2 + h : 3 + h, :] for st in stats]
            top = own[h : h + 1, :]
            for sh in shifts:
                top = jnp.maximum(top, sh)
            own_w = jnp.exp(own[h : h + 1, :] - top)
            ws = [jnp.exp(sh - top) for sh in shifts]
            den = own_w * own[2 + h : 3 + h, :]
            for w, t in zip(ws, totals):
                den = den + w * t
            inv = 1.0 / den
            num = own_acc[u, span, :] * (own_w * inv)
            for (a, c), w in zip(spots, ws):
                first = c * PIECES + h * (PIECES // 2)
                part = jnp.concatenate([ret_in[a, first + i] for i in range(PIECES // 2)], axis=0)
                num = num + part.astype(jnp.float32) * (w * inv)
            rows.append(num)
        result = jnp.concatenate(rows, axis=0)
        rows_at = pl.ds(pl.multiple_of(tile * TILE, TILE), TILE)
        out[rows_at, pl.ds(pl.multiple_of(g * PAIR, PAIR), PAIR)] = result.T.astype(jnp.bfloat16)

    @pl.loop(0, UNITS // 8)
    def _(i):
        for k in range(8):
            combine(8 * i + k)


def local(queries, key_rows, values, tissue, routes):
    wide = jnp.pad(tissue[:, None], ((0, 0), (0, 0), (0, UNITS - tissue.shape[1])))
    small = jnp.concatenate([routes.transpose(0, 2, 1), wide], axis=1)
    vmem = pl.BlockSpec(memory_space=pltpu.VMEM)
    hbm = pl.BlockSpec(memory_space=pltpu.HBM)
    dma = pltpu.SemaphoreType.DMA
    steps = HALF + 1
    rows = (2 * TILE, HP * PAIR)
    block = (HP, 4, PAIR, TILE)
    out = pl.pallas_call(
        kernel,
        out_shape=jax.ShapeDtypeStruct(rows, jnp.bfloat16),
        in_specs=[hbm] * 4,
        out_specs=vmem,
        scratch_shapes=[
            pltpu.SMEM((SPAN + 1, UNITS), jnp.int32),
            pltpu.VMEM(rows, jnp.bfloat16),
            pltpu.VMEM(rows, jnp.bfloat16),
            pltpu.VMEM(rows, jnp.bfloat16),
            pltpu.VMEM((NZ,) + block, jnp.bfloat16),
            pltpu.VMEM((NZ, 2, 8, 128), jnp.int32),
            pltpu.VMEM(block, jnp.bfloat16),
            pltpu.VMEM(block, jnp.bfloat16),
            pltpu.VMEM(block, jnp.bfloat16),
            pltpu.VMEM((NY, UNITS, PAIR, TILE), jnp.bfloat16),
            pltpu.VMEM((NY, 8, 128), jnp.int32),
            pltpu.VMEM((NY, 8, 128), jnp.int32),
            pltpu.SMEM((NY, 8, 128), jnp.int32),
            pltpu.SMEM((NY, 8, 128), jnp.int32),
            pltpu.SMEM((2 * UNITS * SPAN,), jnp.int32),
            pltpu.VMEM((NY, NZ, 2 * PIECES + 1, PIECE, TILE), jnp.bfloat16),
            pltpu.VMEM((NY * NZ, 2 * PIECES + 1, PIECE, TILE), jnp.bfloat16),
            pltpu.VMEM((UNITS, PAIR, TILE), jnp.float32),
            pltpu.VMEM((UNITS, 8, 128), jnp.float32),
            dma((steps, HP)), dma((steps, HP)), dma((steps, HP)), dma((steps, HP)),
            dma((steps,)), dma((steps,)), dma((steps,)), dma((steps,)),
            dma((3, 2)), dma((3, 2)), dma((NY,)), dma((NY,)),
            dma((NY, NZ)), dma((NY, NZ)), dma((6,)),
        ],
        compiler_params=pltpu.CompilerParams(
            collective_id=0, has_side_effects=True, vmem_limit_bytes=53 * 1024 * 1024
        ),
    )(small, queries, key_rows, values)
    return out[None]


def solution(mesh):
    placed = (
        P("slide", "seq", None),
        P("slide", "seq", None),
        P("slide", "seq", None),
        P("slide", "seq"),
        P("slide", "seq", None),
    )
    return jax.shard_map(
        local, mesh=mesh, in_specs=placed, out_specs=P("slide", "seq", None), check_vma=False
    )
```
